32 devices in a mesh: expert: 4 (over z), tok: 8 (over y, x, core).
Axes of the slice: x: 2, y: 2, z: 4, core: 2. Of those that a mesh axis runs over, the one named last changes fastest.
Arguments:
- tokens: bfloat16 [4096, 3072], P(('expert', 'tok')), may hold values from -6 to 6
- grad_out: bfloat16 [4096, 3072], P(('expert', 'tok')), may hold values from -6 to 6
- probs: bfloat16 [4096, 2], P(('expert', 'tok')), may hold values from 0.099609375 to 1
- routes: int32 [32, 2], P(('expert', 'tok')), may hold values from 0 to 3, as said below
- w_gate: bfloat16 [4, 3072, 384], P('expert', 'tok'), may hold values from -0.109375 to 0.109375
- w_up: bfloat16 [4, 3072, 384], P('expert', 'tok'), may hold values from -0.109375 to 0.109375
- w_down_t: bfloat16 [4, 3072, 384], P('expert', 'tok'), may hold values from -0.109375 to 0.109375
Outputs:
- grad_tokens: bfloat16 [4096, 3072], P(('expert', 'tok'))
- grad_probs: bfloat16 [4096, 2], P(('expert', 'tok'))
- grad_gate: float32 [4, 3072, 384], P('expert', 'tok')
- grad_up: float32 [4, 3072, 384], P('expert', 'tok')
- grad_down_t: float32 [4, 3072, 384], P('expert', 'tok')
The draws below stay inside these ranges and needn't reach their ends.
Inputs may be any that keep to these rules, and one draw needn't show every extreme that they name: `routes`: the two experts of a tile differ.
All inputs are finite; a program needn't handle non-finite values.
Results may differ from the reference program's by a relative error of at most 0.0058.
Values may be sent and summed in bfloat16 or wider, within the bound.
A program may use at most 128 MiB of HBM per device.

```python
import jax
import jax.numpy as jnp
from jax import lax

D = 3072
F = 384
TILE = 128
EXPERTS = 4
TILES_DEV = 1
TOKENS = 4096
TILES = 32
N_TOK = 8


def draw_routes(key, part):
    base = jax.random.fold_in(key, 11)
    keys = jax.random.split(base, 6)
    busy = jax.random.randint(keys[0], (), 0, EXPERTS)
    coin = jax.random.randint(keys[1], (TILES,), 0, 8)
    other = (busy + jax.random.randint(keys[2], (TILES,), 1, EXPERTS)) % EXPERTS
    first = jnp.where(coin < 4, busy, other)
    column = jax.random.randint(keys[3], (), 0, N_TOK)
    target = jax.random.randint(keys[4], (), 0, EXPERTS)
    device = jnp.arange(TILES) // TILES_DEV
    forced = device % N_TOK == column
    first = jnp.where(forced, target, first)
    second = (first + jax.random.randint(keys[5], (TILES,), 1, EXPERTS)) % EXPERTS
    return jnp.stack([first, second], axis=1).astype(jnp.int32)


def spiked(result, stream_key, source, target, shards_of, factor):
    def block_of(dim):
        return (jnp.arange(result.shape[dim]) // (result.shape[dim] // shards_of)).reshape((-1,) + (1,) * (result.ndim - 1 - dim))

    near = jax.random.permutation(stream_key, shards_of)[block_of(target)]
    far = (block_of(target) + shards_of // 2) % shards_of
    return jnp.where((block_of(source) == near) | (block_of(source) == far), factor * result, result)


def level_of(rng, shape, cuts, smallest, largest):
    def one(dim, parts):
        steps = jax.random.uniform(jax.random.fold_in(jax.random.fold_in(rng, 6), dim), (parts,), jnp.float32, smallest / len(cuts), largest / len(cuts))
        return jnp.repeat(jnp.exp(steps), shape[dim] // parts).reshape((-1,) + (1,) * (len(shape) - dim - 1))

    factor_of = one(*cuts[0])
    for cut in cuts[1:]:
        factor_of = factor_of * one(*cut)
    return factor_of


def scatter_about(stream_key, dims, width, bound, cuts=(), kind=jnp.bfloat16):
    loudness = level_of(stream_key, dims, cuts, -0.22, 0.18) if cuts else 1.0
    entries = jax.random.normal(stream_key, dims, jnp.float32) * width * loudness
    return jnp.minimum(jnp.maximum(entries, -bound), bound).astype(kind)


def noise_with(rng, dims, deviation, reach, cuts, heavy, held_as=jnp.bfloat16):
    array = deviation * jax.random.normal(rng, dims, jnp.float32)
    if cuts:
        array = array * level_of(rng, dims, cuts, -0.22, 0.18)
    return jnp.clip(spiked(array, jax.random.fold_in(rng, 3), *heavy), -reach, reach).astype(held_as)


def setup_inputs(seed: int = 0) -> dict:
    arg_keys = jax.random.split(jax.random.key(seed), 8)
    tokens = noise_with(arg_keys[0], (TOKENS, D), 1.0, 6.0, ((0, 32),), (0, 1, 32, 2.75))
    grad_out = scatter_about(arg_keys[1], (TOKENS, D), 1.0, 6.0, ((0, 32),))
    probs = jnp.clip(0.099609375 + 0.9003906 * jax.random.uniform(arg_keys[2], (TOKENS, 2), jnp.float32) ** level_of(arg_keys[2], (TOKENS, 2), ((0, 32),), -0.2, 0.2), 0.099609375, 1.0).astype(jnp.bfloat16)
    routes = draw_routes(jax.random.fold_in(arg_keys[7], 71), 0)
    w_gate = scatter_about(arg_keys[4], (EXPERTS, D, F), D ** -0.5, 0.109375, ((0, 4), (1, 8)))
    w_up = scatter_about(arg_keys[5], (EXPERTS, D, F), D ** -0.5, 0.109375, ((0, 4), (1, 8)))
    w_down_t = scatter_about(arg_keys[6], (EXPERTS, D, F), D ** -0.5, 0.109375, ((0, 4), (1, 8)))
    return dict(tokens=tokens, grad_out=grad_out, probs=probs, routes=routes, w_gate=w_gate, w_up=w_up, w_down_t=w_down_t)


def reference(tokens, grad_out, probs, routes, w_gate, w_up, w_down_t):
    route_rows = jnp.repeat(routes, TILE, axis=0)
    prob_values = probs.astype(jnp.float32)

    def per_expert(carry, inputs):
        dx_total, prob_total = carry
        gate_w, up_w, down_w, expert_id = inputs
        chosen = route_rows == expert_id
        weight = jnp.sum(jnp.where(chosen, prob_values, 0.0), axis=1)
        gate_pre = jnp.dot(tokens, gate_w, preferred_element_type=jnp.float32)
        up_pre = jnp.dot(tokens, up_w, preferred_element_type=jnp.float32)
        hidden = jax.nn.silu(gate_pre) * up_pre
        back = jnp.dot(grad_out, down_w, preferred_element_type=jnp.float32)
        score = jnp.sum(hidden * back, axis=1).astype(jnp.bfloat16)
        scaled = (weight[:, None] * hidden).astype(jnp.bfloat16)
        grad_down = jnp.dot(grad_out.T, scaled, preferred_element_type=jnp.float32)
        sigmoid_gate = jax.nn.sigmoid(gate_pre)
        delta_hidden = weight[:, None] * back
        delta_gate = (delta_hidden * up_pre * sigmoid_gate * (1.0 + gate_pre * (1.0 - sigmoid_gate))).astype(jnp.bfloat16)
        delta_up = (delta_hidden * gate_pre * sigmoid_gate).astype(jnp.bfloat16)
        grad_gate = jnp.dot(tokens.T, delta_gate, preferred_element_type=jnp.float32)
        grad_up = jnp.dot(tokens.T, delta_up, preferred_element_type=jnp.float32)
        part = (jnp.dot(delta_gate, gate_w.T, preferred_element_type=jnp.float32)
                + jnp.dot(delta_up, up_w.T, preferred_element_type=jnp.float32)).astype(jnp.bfloat16)
        part = lax.optimization_barrier(part)
        score = lax.optimization_barrier(score)
        dx_total = dx_total + part.astype(jnp.float32)
        prob_total = prob_total + jnp.where(chosen, score.astype(jnp.float32)[:, None], 0.0)
        return (dx_total, prob_total), (grad_gate, grad_up, grad_down)

    start = (jnp.zeros((TOKENS, D), jnp.float32), jnp.zeros((TOKENS, 2), jnp.float32))
    expert_ids = jnp.arange(EXPERTS, dtype=jnp.int32)
    (dx_total, prob_total), grads = lax.scan(per_expert, start, (w_gate, w_up, w_down_t, expert_ids))
    return (dx_total.astype(jnp.bfloat16), prob_total.astype(jnp.bfloat16), grads[0], grads[1], grads[2])
```

```python
import functools

import jax
import jax.numpy as jnp
from jax import lax
from jax.experimental import pallas as pl
from jax.experimental.pallas import tpu as pltpu
from jax.sharding import PartitionSpec as P


def first_section(x_rows, dy_rows, p_rows, gate_w, up_w, down_w):
    gate_pre = jnp.dot(x_rows, gate_w, preferred_element_type=jnp.float32)
    up_pre = jnp.dot(x_rows, up_w, preferred_element_type=jnp.float32)
    hidden = jax.nn.silu(gate_pre) * up_pre
    back = jnp.dot(dy_rows, down_w, preferred_element_type=jnp.float32)
    score = jnp.sum(hidden * back, axis=1).astype(jnp.bfloat16)
    scaled = (p_rows.astype(jnp.float32)[:, None] * hidden).astype(jnp.bfloat16)
    grad_down = lax.dot_general(
        dy_rows, scaled, (((0,), (0,)), ((), ())), preferred_element_type=jnp.float32
    )
    return (gate_pre, up_pre, back, score, grad_down)


def second_section(x_rows, p_rows, gate_pre, up_pre, back, gate_w, up_w):
    sigmoid_gate = jax.nn.sigmoid(gate_pre)
    delta_hidden = p_rows.astype(jnp.float32)[:, None] * back
    delta_gate = (
        delta_hidden * up_pre * sigmoid_gate * (1.0 + gate_pre * (1.0 - sigmoid_gate))
    ).astype(jnp.bfloat16)
    delta_up = (delta_hidden * gate_pre * sigmoid_gate).astype(jnp.bfloat16)
    contract_rows = (((0,), (0,)), ((), ()))
    grad_gate = lax.dot_general(
        x_rows, delta_gate, contract_rows, preferred_element_type=jnp.float32
    )
    grad_up = lax.dot_general(x_rows, delta_up, contract_rows, preferred_element_type=jnp.float32)
    contract_cols = (((1,), (1,)), ((), ()))
    part = (
        lax.dot_general(delta_gate, gate_w, contract_cols, preferred_element_type=jnp.float32)
        + lax.dot_general(delta_up, up_w, contract_cols, preferred_element_type=jnp.float32)
    ).astype(jnp.bfloat16)
    return (grad_gate, grad_up, part)


def on_device(tokens, grad_out, probs, routes, w_gate, w_up, w_down_t):
    groups = lax.axis_size("expert")
    tile_count = routes.shape[0]
    row_count = tokens.shape[0]
    tile_rows = row_count // tile_count
    model_width = tokens.shape[1]
    gate_full, up_full, down_full = (
        lax.all_gather(w_gate, "tok", axis=1, tiled=True),
        lax.all_gather(w_up, "tok", axis=1, tiled=True),
        lax.all_gather(w_down_t, "tok", axis=1, tiled=True),
    )
    gate_w = gate_full[0]
    up_w = up_full[0]
    down_w = down_full[0]
    targets = jnp.arange(groups, dtype=jnp.int32)
    chosen = routes[None, :, :] == targets[:, None, None]
    routed = jnp.any(chosen, axis=2)
    token_tiles = tokens.reshape(tile_count, tile_rows, model_width)
    grad_tiles = grad_out.reshape(tile_count, tile_rows, model_width)
    prob_tiles = probs.reshape(tile_count, tile_rows, 2).astype(jnp.float32)
    x_send = jnp.where(routed[:, :, None, None], token_tiles[None], jnp.zeros((), jnp.bfloat16))
    dy_send = jnp.where(routed[:, :, None, None], grad_tiles[None], jnp.zeros((), jnp.bfloat16))
    p_send = jnp.sum(jnp.where(chosen[:, :, None, :], prob_tiles[None], 0.0), axis=3).astype(
        jnp.bfloat16
    )
    x_recv, dy_recv, p_recv = (
        lax.all_to_all(x_send, "expert", split_axis=0, concat_axis=0, tiled=True),
        lax.all_to_all(dy_send, "expert", split_axis=0, concat_axis=0, tiled=True),
        lax.all_to_all(p_send, "expert", split_axis=0, concat_axis=0, tiled=True),
    )
    slot_count = groups * tile_count
    x_slots = x_recv.reshape(slot_count, tile_rows, model_width)
    dy_slots = dy_recv.reshape(slot_count, tile_rows, model_width)
    p_slots = p_recv.reshape(slot_count, tile_rows)
    total_rows = slot_count * tile_rows
    gate_pre, up_pre, back, score, grad_down = first_section(
        x_slots.reshape(total_rows, model_width),
        dy_slots.reshape(total_rows, model_width),
        p_slots.reshape(total_rows),
        gate_w,
        up_w,
        down_w,
    )
    grad_gate, grad_up, part = second_section(
        x_slots.reshape(total_rows, model_width),
        p_slots.reshape(total_rows),
        gate_pre,
        up_pre,
        back,
        gate_w,
        up_w,
    )
    grad_gate_out, grad_up_out, grad_down_t = (
        lax.psum_scatter(grad_gate[None], "tok", scatter_dimension=1, tiled=True),
        lax.psum_scatter(grad_up[None], "tok", scatter_dimension=1, tiled=True),
        lax.psum_scatter(grad_down[None], "tok", scatter_dimension=1, tiled=True),
    )
    part_send = part.reshape(groups, tile_count, tile_rows, model_width)
    score_send = score.reshape(groups, tile_count, tile_rows)
    part_back, score_back = (
        lax.all_to_all(part_send, "expert", split_axis=0, concat_axis=0, tiled=True),
        lax.all_to_all(score_send, "expert", split_axis=0, concat_axis=0, tiled=True),
    )
    grad_tokens = (
        jnp.sum(part_back.astype(jnp.float32), axis=0)
        .reshape(row_count, model_width)
        .astype(jnp.bfloat16)
    )
    onehot = chosen.astype(jnp.float32)
    grad_probs = jnp.einsum("gtk,gtr->trk", onehot, score_back.astype(jnp.float32))
    grad_probs = grad_probs.reshape(row_count, 2).astype(jnp.bfloat16)
    return (grad_tokens, grad_probs, grad_gate_out, grad_up_out, grad_down_t)


def exchange_kernel(
    nz, nt, x_ref, dy_ref, p_ref, r_ref, wg_ref, wu_ref, wd_ref,
    gt_ref, score_ref, gg_ref, gu_ref, gd_ref,
    xs, dys, rt, x_t, dy_t, wall, acc, sib, comb, pin, pre, dall, picked, gsc, rout, rin, rin2, pt,
    xsend, xrecv, dsend, drecv, rsend, rrecv, wsend, wrecv, csend, crecv, hsend, hrecv,
    asend, arecv, zsend, zrecv, zrecv2, psend, precv,
):
    f32, bf16 = jnp.float32, jnp.bfloat16
    z, me = lax.axis_index("expert"), lax.axis_index("tok")
    chips = nt // 2
    chip, core = me // 2, lax.rem(me, 2)
    mine = core * chips + chip
    sibling = 2 * chip + 1 - core
    rows, ds, f = xs.shape[1], xs.shape[2], wg_ref.shape[2]
    weights = (wg_ref, wu_ref, wd_ref)
    grads = (gg_ref, gu_ref, gd_ref)
    pending = []

    def slot_of(tok):
        return lax.rem(tok, 2) * chips + tok // 2

    def partner(j):
        return lax.rem(chip + j, chips)

    def move(src, dst, send, recv, zz, tok):
        return pltpu.make_async_remote_copy(
            src_ref=src, dst_ref=dst, send_sem=send, recv_sem=recv,
            device_id=(zz, tok), device_id_type=pl.DeviceIdType.MESH,
        )

    def start(cond, *args):
        copy = move(*args)
        if cond is None:
            copy.start()
        else:
            pl.when(cond)(lambda: copy.start())
        pending.append((cond, copy))

    def arrived(dst, recv):
        move(dst, dst, xsend.at[0], recv, z, sibling).wait_recv()

    barrier = pltpu.get_barrier_semaphore()
    for r in range(1, nt):
        pl.semaphore_signal(
            barrier, inc=1, device_id=(z, lax.rem(me + r, nt)), device_id_type=pl.DeviceIdType.MESH
        )

    @pl.when(z > 0)
    def _():
        pl.semaphore_signal(barrier, inc=1, device_id=(z - 1, me), device_id_type=pl.DeviceIdType.MESH)

    @pl.when(z < nz - 1)
    def _():
        pl.semaphore_signal(barrier, inc=1, device_id=(z + 1, me), device_id_type=pl.DeviceIdType.MESH)

    inner = jnp.where(z > 0, 1, 0) + jnp.where(z < nz - 1, 1, 0)
    pl.semaphore_wait(barrier, nt - 1 + inner)

    def send_weight(m, d):
        src_r = weights[m].at[0] if d == 0 else wall.at[m, z - d]
        src_l = weights[m].at[0] if d == 0 else wall.at[m, z + d]
        base = m * 2 * nz + d
        start((z - d >= 0) & (z < nz - 1), src_r, wall.at[m, z - d], wsend.at[base],
              wrecv.at[m * nz + z - d], z + 1, me)
        start((z + d < nz) & (z > 0), src_l, wall.at[m, z + d], wsend.at[base + nz],
              wrecv.at[m * nz + z + d], z - 1, me)

    def send_rows(src_ref, dst, send, recv):
        for r in range(1, nt):
            t = lax.rem(me + r, nt)
            cols = pl.ds(pl.multiple_of(t * ds, ds), ds)
            start(None, src_ref.at[:, cols], dst.at[mine], send.at[r], recv.at[mine], z, t)

    own_cols = pl.ds(pl.multiple_of(me * ds, ds), ds)
    send_weight(0, 0)
    for r in range(1, nt):
        t = lax.rem(me + r, nt)
        start(None, r_ref, rt.at[mine], rsend.at[r], rrecv.at[mine], z, t)
    send_rows(x_ref, xs, xsend, xrecv)
    send_weight(1, 0)
    send_rows(dy_ref, dys, dsend, drecv)
    for m in range(3):
        wall[m, z] = weights[m][0]
    rt[mine] = r_ref[...]
    xs[mine] = x_ref[:, own_cols]
    dys[mine] = dy_ref[:, own_cols]

    def take_rows(dst, recv):
        for r in range(1, nt):
            s = slot_of(lax.rem(me + r, nt))
            arrived(dst.at[s], recv.at[s])

    def hits(i, k, e):
        return jnp.broadcast_to(rt[pl.ds(2 * i, 2), k : k + 1, :], (2, rows, f)) == e

    def project(m, src, e, first):
        @pl.loop(0, nt // 2)
        def _(i):
            block = src[pl.ds(2 * i, 2)].reshape(2 * rows, ds)
            out = jnp.dot(block, wall[m, e], preferred_element_type=f32).reshape(2, rows, f)
            for k in range(2):
                old = jnp.zeros((2, rows, f), f32) if first else acc[m, pl.ds(2 * i, 2), k]
                acc[m, pl.ds(2 * i, 2), k] = jnp.where(hits(i, k, e), out, old)

    def take_weight(m, d):
        pl.when(z - d >= 0)(lambda: arrived(wall.at[m, z - d], wrecv.at[m * nz + z - d]))
        pl.when(z + d < nz)(lambda: arrived(wall.at[m, z + d], wrecv.at[m * nz + z + d]))
        if d < nz - 1:
            send_weight(m, d)

    def far_projects(m, src, d):
        pl.when(z - d >= 0)(lambda: project(m, src, z - d, False))
        pl.when(z + d < nz)(lambda: project(m, src, z + d, False))

    def cores_send(m):
        start(None, acc.at[m, pl.ds((1 - core) * chips, chips)], sib.at[m], csend.at[m], crecv.at[m], z, sibling)

    def chips_send(m):
        arrived(sib.at[m], crecv.at[m])
        for j in range(1, chips):
            q = partner(j)
            comb[m, q] = (acc[m, core * chips + q] + sib[m, q]).astype(bf16)
            n = m * chips + j
            start(None, comb.at[m, q], pin.at[m, chip], hsend.at[n], hrecv.at[m * chips + chip], z, 2 * q + core)

    def home(m):
        for j in range(1, chips):
            q = partner(j)
            arrived(pin.at[m, q], hrecv.at[m * chips + q])
        for k in range(2):
            total = acc[m, mine, k] + sib[m, chip, k]
            for j in range(1, chips):
                total = total + pin[m, partner(j), k].astype(f32)
            pre[m, k] = total

    def spread(m):
        for j in range(1, chips):
            q = partner(j)
            start(None, dall.at[m, mine], dall.at[m, mine], asend.at[m * nt + j], arecv.at[m * nt + mine],
                  z, 2 * q + core)
        start(None, dall.at[m, mine], dall.at[m, mine], asend.at[m * nt], arecv.at[m * nt + mine], z, sibling)

    def relay(m):
        for j in range(1, chips):
            s = core * chips + partner(j)
            arrived(dall.at[m, s], arecv.at[m * nt + s])
            start(None, dall.at[m, s], dall.at[m, s], asend.at[m * nt + chips + j], arecv.at[m * nt + s], z, sibling)

    def gathered(m):
        for q in range(chips):
            s = (1 - core) * chips + q
            arrived(dall.at[m, s], arecv.at[m * nt + s])

    def pick(m, which):
        @pl.loop(0, nt // 2)
        def _(i):
            one = dall[m, pl.ds(2 * i, 2), 0].astype(f32)
            two = dall[m, pl.ds(2 * i, 2), 1].astype(f32)
            for e in range(nz):
                value = jnp.where(hits(i, 0, e), one, jnp.where(hits(i, 1, e), two, 0.0))
                picked[which, e, pl.ds(2 * i, 2)] = value.astype(bf16)

    def grad_of(lhs, which, e):
        gsc[...] = jnp.dot(lhs[...], picked[which, e].reshape(nt * rows, f), preferred_element_type=f32)

    def chain(m, lhs, which, d):
        @pl.when(z + d < nz)
        def _():
            e = z + d
            grad_of(lhs, which, e)

            @pl.when(z > 0)
            def _():
                arrived(rin.at[m, e], zrecv.at[m * nz + e])
                gsc[...] += rin[m, e].astype(f32)

            rout[m, e] = gsc[...].astype(bf16)

        start(z + d < nz, rout.at[m, z + d], rin.at[m, z + d], zsend.at[m * 2 * nz + d],
              zrecv.at[m * nz + z + d], z + 1, me)

        @pl.when(z - d >= 0)
        def _():
            e = z - d
            grad_of(lhs, which, e)

            @pl.when(z < nz - 1)
            def _():
                arrived(rin.at[m, e], zrecv.at[m * nz + e])
                gsc[...] += rin[m, e].astype(f32)

            rout[m, e] = gsc[...].astype(bf16)

        dst = rin2.at[m] if d == 1 else rin.at[m, z - d]
        sem = zrecv2.at[m] if d == 1 else zrecv.at[m * nz + z - d]
        start(z - d >= 0, rout.at[m, z - d], dst, zsend.at[m * 2 * nz + nz + d], sem, z - 1, me)

    def finish(m):
        out = grads[m]

        @pl.when(z > 0)
        def _():
            arrived(rin.at[m, z], zrecv.at[m * nz + z])
            out[0] += rin[m, z].astype(f32)

        @pl.when(z < nz - 1)
        def _():
            arrived(rin2.at[m], zrecv2.at[m])
            out[0] += rin2[m].astype(f32)

    def own_grad(m, lhs, which):
        grad_of(lhs, which, z)
        grads[m][0] = gsc[...]

    def transpose(src, dst):
        for t in range(nt):
            dst[:, t * rows : (t + 1) * rows] = src[t].T

    take_rows(rt, rrecv)
    take_rows(xs, xrecv)
    project(0, xs, z, True)
    take_weight(0, 1)
    project(1, xs, z, True)
    far_projects(0, xs, 1)
    take_weight(0, 2)
    send_weight(2, 0)
    far_projects(0, xs, 2)
    take_rows(dys, drecv)
    take_weight(0, 3) if nz > 3 else None
    far_projects(0, xs, 3) if nz > 3 else None
    cores_send(0)
    take_weight(1, 1)
    project(2, dys, z, True)
    far_projects(1, xs, 1)
    chips_send(0)
    take_weight(1, 2)
    far_projects(1, xs, 2)
    transpose(dys, dy_t)
    take_weight(1, 3) if nz > 3 else None
    far_projects(1, xs, 3) if nz > 3 else None
    cores_send(1)
    take_weight(2, 1)
    far_projects(2, dys, 1)
    chips_send(1)
    home(0)
    take_weight(2, 2)
    far_projects(2, dys, 2)
    home(1)
    for k in range(2):
        g, u = pre[0, k], pre[1, k]
        dall[0, mine, k] = (p_ref[k] * (g * jax.nn.sigmoid(g) * u)).astype(bf16)
    spread(0)
    transpose(xs, x_t)
    take_weight(2, 3) if nz > 3 else None
    far_projects(2, dys, 3) if nz > 3 else None
    cores_send(2)
    relay(0)
    chips_send(2)
    gathered(0)
    pick(0, 0)
    home(2)
    for k in range(2):
        g, u, b = pre[0, k], pre[1, k], pre[2, k]
        s = jax.nn.sigmoid(g)
        score_ref[k] = jnp.sum(g * s * u * b, axis=1, keepdims=True)
        scaled_back = p_ref[k] * b
        dall[1, mine, k] = (scaled_back * u * s * (1.0 + g * (1.0 - s))).astype(bf16)
        dall[2, mine, k] = (scaled_back * g * s).astype(bf16)
    spread(1)
    spread(2)
    for d in range(nz - 1, 1, -1):
        chain(2, dy_t, 0, d)
    relay(1)
    chain(2, dy_t, 0, 1)
    relay(2)
    own_grad(2, dy_t, 0)
    gathered(1)
    pick(1, 0)
    chain(0, x_t, 0, nz - 1)
    gathered(2)
    pick(2, 1)
    chain(1, x_t, 1, nz - 1)
    for d in range(nz - 2, 0, -1):
        chain(0, x_t, 0, d)
        chain(1, x_t, 1, d)

    @pl.loop(0, nt // 2)
    def _(i):
        total = jnp.zeros((2 * rows, ds), f32)
        for e in range(nz):
            for m in range(2):
                block = picked[m, e, pl.ds(2 * i, 2)].reshape(2 * rows, f)
                total = total + lax.dot_general(
                    block, wall[m, e], (((1,), (1,)), ((), ())), preferred_element_type=f32
                )
        pt[pl.ds(2 * i, 2)] = total.reshape(2, rows, ds).astype(bf16)

    for r in range(1, nt):
        t = lax.rem(me + r, nt)
        start(None, pt.at[slot_of(t)], gt_ref.at[:, own_cols], psend.at[r], precv.at[mine], z, t)
    gt_ref[:, own_cols] = pt[mine]
    own_grad(0, x_t, 0)
    own_grad(1, x_t, 1)
    finish(2)
    for r in range(1, nt):
        t = lax.rem(me + r, nt)
        cols = pl.ds(pl.multiple_of(t * ds, ds), ds)
        arrived(gt_ref.at[:, cols], precv.at[slot_of(t)])
    finish(0)
    finish(1)
    for cond, copy in pending:
        if cond is None:
            copy.wait_send()
        else:
            pl.when(cond)(copy.wait_send)


def on_device_kernel(nz, nt, tokens, grad_out, probs, routes, w_gate, w_up, w_down_t):
    rows, width = tokens.shape
    ds, f = w_gate.shape[1], w_gate.shape[2]
    f32, bf16 = jnp.float32, jnp.bfloat16
    weight = probs.astype(f32).T[:, :, None]
    route = jnp.broadcast_to(jnp.pad(routes[0], (0, 6))[:, None], (8, f))
    chips = nt // 2
    vmem, dma = pltpu.VMEM, pltpu.SemaphoreType.DMA
    grad = jax.ShapeDtypeStruct((1, ds, f), f32)
    flops = 2 * nt * rows * ds * f * nz * 8
    out = pl.pallas_call(
        functools.partial(exchange_kernel, nz, nt),
        out_shape=(
            jax.ShapeDtypeStruct((rows, width), bf16),
            jax.ShapeDtypeStruct((2, rows, 1), f32),
            grad, grad, grad,
        ),
        in_specs=[pl.BlockSpec(memory_space=vmem)] * 7,
        out_specs=[pl.BlockSpec(memory_space=vmem)] * 5,
        scratch_shapes=[
            vmem((nt, rows, ds), bf16), vmem((nt, rows, ds), bf16), vmem((nt, 8, f), jnp.int32),
            vmem((ds, nt * rows), bf16), vmem((ds, nt * rows), bf16),
            vmem((3, nz, ds, f), bf16),
            vmem((3, nt, 2, rows, f), f32),
            vmem((3, chips, 2, rows, f), f32),
            vmem((3, chips, 2, rows, f), bf16),
            vmem((3, chips, 2, rows, f), bf16),
            vmem((3, 2, rows, f), f32),
            vmem((3, nt, 2, rows, f), bf16),
            vmem((2, nz, nt, rows, f), bf16),
            vmem((ds, f), f32),
            vmem((3, nz, ds, f), bf16), vmem((3, nz, ds, f), bf16), vmem((3, ds, f), bf16),
            vmem((nt, rows, ds), bf16),
            dma((nt,)), dma((nt,)), dma((nt,)), dma((nt,)), dma((nt,)), dma((nt,)),
            dma((6 * nz,)), dma((3 * nz,)),
            dma((3,)), dma((3,)),
            dma((3 * chips,)), dma((3 * chips,)),
            dma((3 * nt,)), dma((3 * nt,)),
            dma((6 * nz,)), dma((3 * nz,)), dma((3,)),
            dma((nt,)), dma((nt,)),
        ],
        compiler_params=pltpu.CompilerParams(
            collective_id=0, has_side_effects=True, vmem_limit_bytes=62 * 2**20
        ),
        cost_estimate=pl.CostEstimate(flops=flops, bytes_accessed=2**23, transcendentals=0),
    )(tokens, grad_out, weight, route, w_gate, w_up, w_down_t)
    grad_probs = out[1][:, :, 0].T.astype(bf16)
    return (out[0], grad_probs, out[2], out[3], out[4])


def fits(mesh, tokens, routes, w_gate):
    nz, nt = mesh.shape["expert"], mesh.shape["tok"]
    devices = nz * nt
    rows, ds, f = tokens.shape[0] // devices, w_gate.shape[1] // nt, w_gate.shape[2]
    if routes.shape[0] != devices or w_gate.shape[0] != nz or nz != 4 or nt % 2:
        return False
    if rows % 16 or ds % 128 or f % 128 or nt > 8:
        return False
    return nt * rows * f <= 8 * 128 * 384 and ds * f <= 384 * 384


def solution(mesh):
    def run(tokens, grad_out, probs, routes, w_gate, w_up, w_down_t):
        body = on_device
        if fits(mesh, tokens, routes, w_gate):
            body = functools.partial(on_device_kernel, mesh.shape["expert"], mesh.shape["tok"])
        rows = P(("expert", "tok"), None)
        weights = P("expert", "tok", None)
        return jax.shard_map(
            body,
            mesh=mesh,
            in_specs=(rows, rows, rows, rows, weights, weights, weights),
            out_specs=(rows, rows, weights, weights, weights),
            check_vma=False,
        )(tokens, grad_out, probs, routes, w_gate, w_up, w_down_t)

    return run
```

```python
import functools

import jax
import jax.numpy as jnp
from jax import lax
from jax.experimental import pallas as pl
from jax.experimental.pallas import tpu as pltpu
from jax.sharding import PartitionSpec as P


def first_section(x_rows, dy_rows, p_rows, gate_w, up_w, down_w):
    gate_pre = jnp.dot(x_rows, gate_w, preferred_element_type=jnp.float32)
    up_pre = jnp.dot(x_rows, up_w, preferred_element_type=jnp.float32)
    hidden = jax.nn.silu(gate_pre) * up_pre
    back = jnp.dot(dy_rows, down_w, preferred_element_type=jnp.float32)
    score = jnp.sum(hidden * back, axis=1).astype(jnp.bfloat16)
    scaled = (p_rows.astype(jnp.float32)[:, None] * hidden).astype(jnp.bfloat16)
    grad_down = lax.dot_general(
        dy_rows, scaled, (((0,), (0,)), ((), ())), preferred_element_type=jnp.float32
    )
    return (gate_pre, up_pre, back, score, grad_down)


def second_section(x_rows, p_rows, gate_pre, up_pre, back, gate_w, up_w):
    sigmoid_gate = jax.nn.sigmoid(gate_pre)
    delta_hidden = p_rows.astype(jnp.float32)[:, None] * back
    delta_gate = (
        delta_hidden * up_pre * sigmoid_gate * (1.0 + gate_pre * (1.0 - sigmoid_gate))
    ).astype(jnp.bfloat16)
    delta_up = (delta_hidden * gate_pre * sigmoid_gate).astype(jnp.bfloat16)
    contract_rows = (((0,), (0,)), ((), ()))
    grad_gate = lax.dot_general(
        x_rows, delta_gate, contract_rows, preferred_element_type=jnp.float32
    )
    grad_up = lax.dot_general(x_rows, delta_up, contract_rows, preferred_element_type=jnp.float32)
    contract_cols = (((1,), (1,)), ((), ()))
    part = (
        lax.dot_general(delta_gate, gate_w, contract_cols, preferred_element_type=jnp.float32)
        + lax.dot_general(delta_up, up_w, contract_cols, preferred_element_type=jnp.float32)
    ).astype(jnp.bfloat16)
    return (grad_gate, grad_up, part)


def on_device(tokens, grad_out, probs, routes, w_gate, w_up, w_down_t):
    groups = lax.axis_size("expert")
    tile_count = routes.shape[0]
    row_count = tokens.shape[0]
    tile_rows = row_count // tile_count
    model_width = tokens.shape[1]
    gate_full, up_full, down_full = (
        lax.all_gather(w_gate, "tok", axis=1, tiled=True),
        lax.all_gather(w_up, "tok", axis=1, tiled=True),
        lax.all_gather(w_down_t, "tok", axis=1, tiled=True),
    )
    gate_w = gate_full[0]
    up_w = up_full[0]
    down_w = down_full[0]
    targets = jnp.arange(groups, dtype=jnp.int32)
    chosen = routes[None, :, :] == targets[:, None, None]
    routed = jnp.any(chosen, axis=2)
    token_tiles = tokens.reshape(tile_count, tile_rows, model_width)
    grad_tiles = grad_out.reshape(tile_count, tile_rows, model_width)
    prob_tiles = probs.reshape(tile_count, tile_rows, 2).astype(jnp.float32)
    x_send = jnp.where(routed[:, :, None, None], token_tiles[None], jnp.zeros((), jnp.bfloat16))
    dy_send = jnp.where(routed[:, :, None, None], grad_tiles[None], jnp.zeros((), jnp.bfloat16))
    p_send = jnp.sum(jnp.where(chosen[:, :, None, :], prob_tiles[None], 0.0), axis=3).astype(
        jnp.bfloat16
    )
    x_recv, dy_recv, p_recv = (
        lax.all_to_all(x_send, "expert", split_axis=0, concat_axis=0, tiled=True),
        lax.all_to_all(dy_send, "expert", split_axis=0, concat_axis=0, tiled=True),
        lax.all_to_all(p_send, "expert", split_axis=0, concat_axis=0, tiled=True),
    )
    slot_count = groups * tile_count
    x_slots = x_recv.reshape(slot_count, tile_rows, model_width)
    dy_slots = dy_recv.reshape(slot_count, tile_rows, model_width)
    p_slots = p_recv.reshape(slot_count, tile_rows)
    total_rows = slot_count * tile_rows
    gate_pre, up_pre, back, score, grad_down = first_section(
        x_slots.reshape(total_rows, model_width),
        dy_slots.reshape(total_rows, model_width),
        p_slots.reshape(total_rows),
        gate_w,
        up_w,
        down_w,
    )
    grad_gate, grad_up, part = second_section(
        x_slots.reshape(total_rows, model_width),
        p_slots.reshape(total_rows),
        gate_pre,
        up_pre,
        back,
        gate_w,
        up_w,
    )
    grad_gate_out, grad_up_out, grad_down_t = (
        lax.psum_scatter(grad_gate[None], "tok", scatter_dimension=1, tiled=True),
        lax.psum_scatter(grad_up[None], "tok", scatter_dimension=1, tiled=True),
        lax.psum_scatter(grad_down[None], "tok", scatter_dimension=1, tiled=True),
    )
    part_send = part.reshape(groups, tile_count, tile_rows, model_width)
    score_send = score.reshape(groups, tile_count, tile_rows)
    part_back, score_back = (
        lax.all_to_all(part_send, "expert", split_axis=0, concat_axis=0, tiled=True),
        lax.all_to_all(score_send, "expert", split_axis=0, concat_axis=0, tiled=True),
    )
    grad_tokens = (
        jnp.sum(part_back.astype(jnp.float32), axis=0)
        .reshape(row_count, model_width)
        .astype(jnp.bfloat16)
    )
    onehot = chosen.astype(jnp.float32)
    grad_probs = jnp.einsum("gtk,gtr->trk", onehot, score_back.astype(jnp.float32))
    grad_probs = grad_probs.reshape(row_count, 2).astype(jnp.bfloat16)
    return (grad_tokens, grad_probs, grad_gate_out, grad_up_out, grad_down_t)


LANES = 128

def exchange_kernel(
    nz, nt, x_ref, dy_ref, p_ref, r_ref, wg_ref, wu_ref, wd_ref,
    gt_ref, score_ref, gg_ref, gu_ref, gd_ref,
    xs, dys, rt, x_t, dy_t, own, wall, acc, sib, comb, pin, dall, picked, gp, rout, rin, rin2, pt, ptf,
    xsend, xrecv, dsend, drecv, rsend, rrecv, wsend, wrecv, csend, crecv, hsend, hrecv,
    asend, arecv, zsend, zrecv, zrecv2, psend, precv,
):
    f32, bf16 = jnp.float32, jnp.bfloat16
    z, me = lax.axis_index("expert"), lax.axis_index("tok")
    chips = nt // 2
    chip, core = me // 2, lax.rem(me, 2)
    mine = core * chips + chip
    sibling = 2 * chip + 1 - core
    rows, ds, f = xs.shape[1], xs.shape[2], wg_ref.shape[2]
    fc = LANES
    parts, bw = f // fc, 3 * fc
    weights = (wg_ref, wu_ref, wd_ref)
    grads = (gg_ref, gu_ref, gd_ref)
    pending = []
    for c in range(parts):
        for m in range(3):
            own[c, :, m * fc : (m + 1) * fc] = weights[m][0, :, c * fc : (c + 1) * fc]

    def slot_of(tok):
        return lax.rem(tok, 2) * chips + tok // 2

    def partner(j):
        return lax.rem(chip + j, chips)

    def move(src, dst, send, recv, zz, tok):
        return pltpu.make_async_remote_copy(
            src_ref=src, dst_ref=dst, send_sem=send, recv_sem=recv,
            device_id=(zz, tok), device_id_type=pl.DeviceIdType.MESH,
        )

    def start(cond, *args):
        copy = move(*args)
        if cond is None:
            copy.start()
        else:
            pl.when(cond)(lambda: copy.start())
        pending.append((cond, copy))

    def arrived(dst, recv):
        move(dst, dst, xsend.at[0], recv, z, sibling).wait_recv()

    barrier = pltpu.get_barrier_semaphore()
    for r in range(1, nt):
        pl.semaphore_signal(
            barrier, inc=1, device_id=(z, lax.rem(me + r, nt)), device_id_type=pl.DeviceIdType.MESH
        )

    @pl.when(z > 0)
    def _():
        pl.semaphore_signal(barrier, inc=1, device_id=(z - 1, me), device_id_type=pl.DeviceIdType.MESH)

    @pl.when(z < nz - 1)
    def _():
        pl.semaphore_signal(barrier, inc=1, device_id=(z + 1, me), device_id_type=pl.DeviceIdType.MESH)

    inner = jnp.where(z > 0, 1, 0) + jnp.where(z < nz - 1, 1, 0)
    pl.semaphore_wait(barrier, nt - 1 + inner)

    def from_left(d):
        return (z - d >= 0) & (z < nz - 1)

    def from_right(d):
        return (z + d < nz) & (z > 0)

    def send_weight(c, d):
        src_r = own.at[c] if d == 0 else wall.at[c, z - d]
        src_l = own.at[c] if d == 0 else wall.at[c, z + d]
        base = c * 2 * nz + d
        start(from_left(d), src_r, wall.at[c, z - d], wsend.at[base], wrecv.at[c * nz + z - d], z + 1, me)
        start(from_right(d), src_l, wall.at[c, z + d], wsend.at[base + nz], wrecv.at[c * nz + z + d], z - 1, me)

    def weight_left(c, d):
        arrived(wall.at[c, z - d], wrecv.at[c * nz + z - d])

    def weight_right(c, d):
        arrived(wall.at[c, z + d], wrecv.at[c * nz + z + d])

    def forward(c, d):
        pl.when(from_left(d))(lambda: weight_left(c, d))
        pl.when(from_right(d))(lambda: weight_right(c, d))
        send_weight(c, d)

    def take_weight(c, d):
        pl.when((z - d >= 0) & ((z == nz - 1) | (d == nz - 1)))(lambda: weight_left(c, d))
        pl.when((z + d < nz) & ((z == 0) | (d == nz - 1)))(lambda: weight_right(c, d))

    def send_rows(src_ref, dst, send, recv):
        for r in range(1, nt):
            t = lax.rem(me + r, nt)
            cols = pl.ds(pl.multiple_of(t * ds, ds), ds)
            start(None, src_ref.at[:, cols], dst.at[mine], send.at[r], recv.at[mine], z, t)

    own_cols = pl.ds(pl.multiple_of(me * ds, ds), ds)
    send_weight(0, 0)
    for r in range(1, nt):
        t = lax.rem(me + r, nt)
        start(None, r_ref, rt.at[mine], rsend.at[r], rrecv.at[mine], z, t)
    send_rows(x_ref, xs, xsend, xrecv)
    send_rows(dy_ref, dys, dsend, drecv)
    for c in range(parts):
        wall[c, z] = own[c]
    rt[mine] = r_ref[...]
    xs[mine] = x_ref[:, own_cols]
    dys[mine] = dy_ref[:, own_cols]

    def take_rows(dst, recv):
        for r in range(1, nt):
            s = slot_of(lax.rem(me + r, nt))
            arrived(dst.at[s], recv.at[s])

    def hits(i, k, e):
        return jnp.broadcast_to(rt[pl.ds(2 * i, 2), k : k + 1, :], (2, rows, bw)) == e

    def project(c, e, first):
        @pl.loop(0, nt // 2)
        def _(i):
            x = xs[pl.ds(2 * i, 2)].reshape(2 * rows, ds)
            dy = dys[pl.ds(2 * i, 2)].reshape(2 * rows, ds)
            up = jnp.dot(x, wall[c, e, :, : 2 * fc], preferred_element_type=f32)
            back = jnp.dot(dy, wall[c, e, :, 2 * fc :], preferred_element_type=f32)
            out = jnp.concatenate([up, back], axis=1).reshape(2, rows, bw)
            for k in range(2):
                old = jnp.zeros((2, rows, bw), f32) if first else acc[c, pl.ds(2 * i, 2), k]
                acc[c, pl.ds(2 * i, 2), k] = jnp.where(hits(i, k, e), out, old)

    def projects(c, d):
        if d == 0:
            project(c, z, True)
            return
        take_weight(c, d)
        pl.when(z - d >= 0)(lambda: project(c, z - d, False))
        pl.when(z + d < nz)(lambda: project(c, z + d, False))

    def cores_send(m):
        start(None, acc.at[m, pl.ds((1 - core) * chips, chips)], sib.at[m], csend.at[m], crecv.at[m], z, sibling)

    def chips_send(m):
        arrived(sib.at[m], crecv.at[m])
        for j in range(1, chips):
            q = partner(j)
            comb[m, q] = (acc[m, core * chips + q] + sib[m, q]).astype(bf16)
            n = m * chips + j
            start(None, comb.at[m, q], pin.at[m, chip], hsend.at[n], hrecv.at[m * chips + chip], z, 2 * q + core)

    def home(c):
        for j in range(1, chips):
            q = partner(j)
            arrived(pin.at[c, q], hrecv.at[c * chips + q])
        for k in range(2):
            total = acc[c, mine, k] + sib[c, chip, k]
            for j in range(1, chips):
                total = total + pin[c, partner(j), k].astype(f32)
            g, u, b = total[:, :fc], total[:, fc : 2 * fc], total[:, 2 * fc :]
            s = jax.nn.sigmoid(g)
            hidden = g * s * u
            score = jnp.sum(hidden * b, axis=1, keepdims=True)
            score_ref[k] = score if c == 0 else score_ref[k] + score
            scaled_back = p_ref[k] * b
            dall[c, mine, k, :, :fc] = (scaled_back * u * s * (1.0 + g * (1.0 - s))).astype(bf16)
            dall[c, mine, k, :, fc : 2 * fc] = (scaled_back * g * s).astype(bf16)
            dall[c, mine, k, :, 2 * fc :] = (p_ref[k] * hidden).astype(bf16)

    def spread(m):
        for j in range(1, chips):
            q = partner(j)
            start(None, dall.at[m, mine], dall.at[m, mine], asend.at[m * nt + j], arecv.at[m * nt + mine],
                  z, 2 * q + core)
        start(None, dall.at[m, mine], dall.at[m, mine], asend.at[m * nt], arecv.at[m * nt + mine], z, sibling)

    def relay(m):
        for j in range(1, chips):
            s = core * chips + partner(j)
            arrived(dall.at[m, s], arecv.at[m * nt + s])
            start(None, dall.at[m, s], dall.at[m, s], asend.at[m * nt + chips + j], arecv.at[m * nt + s], z, sibling)

    def gathered(m):
        for q in range(chips):
            s = (1 - core) * chips + q
            arrived(dall.at[m, s], arecv.at[m * nt + s])

    def pick(c):
        @pl.loop(0, nt // 2)
        def _(i):
            one = dall[c, pl.ds(2 * i, 2), 0].astype(f32)
            two = dall[c, pl.ds(2 * i, 2), 1].astype(f32)
            for e in range(nz):
                value = jnp.where(hits(i, 0, e), one, jnp.where(hits(i, 1, e), two, 0.0))
                picked[e, pl.ds(2 * i, 2)] = value.astype(bf16)

    def grad_of(c, e):
        up = picked[e, :, :, : 2 * fc].reshape(nt * rows, 2 * fc)
        down = picked[e, :, :, 2 * fc :].reshape(nt * rows, fc)
        gp[c % 2, e, :, : 2 * fc] = jnp.dot(x_t[...], up, preferred_element_type=f32)
        gp[c % 2, e, :, 2 * fc :] = jnp.dot(dy_t[...], down, preferred_element_type=f32)

    def chain(c, d):
        @pl.when(z + d < nz)
        def _():
            e = z + d

            @pl.when(z > 0)
            def _():
                arrived(rin.at[c, e], zrecv.at[c * nz + e])
                rout[c, e] = (gp[c % 2, e] + rin[c, e].astype(f32)).astype(bf16)

            @pl.when(z == 0)
            def _():
                rout[c, e] = gp[c % 2, e].astype(bf16)

        start(z + d < nz, rout.at[c, z + d], rin.at[c, z + d], zsend.at[c * 2 * nz + d],
              zrecv.at[c * nz + z + d], z + 1, me)

        @pl.when(z - d >= 0)
        def _():
            e = z - d

            @pl.when(z < nz - 1)
            def _():
                arrived(rin.at[c, e], zrecv.at[c * nz + e])
                rout[c, e] = (gp[c % 2, e] + rin[c, e].astype(f32)).astype(bf16)

            @pl.when(z == nz - 1)
            def _():
                rout[c, e] = gp[c % 2, e].astype(bf16)

        dst = rin2.at[c] if d == 1 else rin.at[c, z - d]
        sem = zrecv2.at[c] if d == 1 else zrecv.at[c * nz + z - d]
        start(z - d >= 0, rout.at[c, z - d], dst, zsend.at[c * 2 * nz + nz + d], sem, z - 1, me)

    def grads_of(c):
        gathered(c)
        pick(c)
        for d in range(nz - 1, 0, -1):
            pl.when(z + d < nz)(lambda d=d: grad_of(c, z + d))
            pl.when(z - d >= 0)(lambda d=d: grad_of(c, z - d))
            if d == nz - 1:
                chain(c, d)
        grad_of(c, z)
        for m in range(3):
            grads[m][0, :, c * fc : (c + 1) * fc] = gp[c % 2, z, :, m * fc : (m + 1) * fc]

        @pl.loop(0, nt // 2)
        def _(i):
            total = jnp.zeros((2 * rows, ds), f32)
            for e in range(nz):
                block = picked[e, pl.ds(2 * i, 2), :, : 2 * fc].reshape(2 * rows, 2 * fc)
                total = total + lax.dot_general(
                    block, wall[c, e, :, : 2 * fc], (((1,), (1,)), ((), ())), preferred_element_type=f32
                )
            total = total.reshape(2, rows, ds)
            if c > 0:
                total = total + ptf[pl.ds(2 * i, 2)]
            if c < parts - 1:
                ptf[pl.ds(2 * i, 2)] = total
            else:
                pt[pl.ds(2 * i, 2)] = total.astype(bf16)

    def finish(c):
        @pl.when(z > 0)
        def _():
            arrived(rin.at[c, z], zrecv.at[c * nz + z])
            for m in range(3):
                grads[m][0, :, c * fc : (c + 1) * fc] += rin[c, z, :, m * fc : (m + 1) * fc].astype(f32)

        @pl.when(z < nz - 1)
        def _():
            arrived(rin2.at[c], zrecv2.at[c])
            for m in range(3):
                grads[m][0, :, c * fc : (c + 1) * fc] += rin2[c, :, m * fc : (m + 1) * fc].astype(f32)

    def transpose(src, dst):
        for t in range(nt):
            dst[:, t * rows : (t + 1) * rows] = src[t].T

    far = nz - 1

    def ahead(c, d):
        if c < parts and d < far:
            forward(c, d)
        if c + 1 < parts and d == far - 1:
            send_weight(c + 1, 0)

    for d in range(1, far):
        ahead(0, d)
    take_rows(rt, rrecv)
    take_rows(xs, xrecv)
    take_rows(dys, drecv)
    for d in range(far):
        projects(0, d)
    for c in range(parts):
        ahead(c + 1, 1)
        projects(c, far)
        cores_send(c)
        if c == 0:
            transpose(xs, x_t)
            transpose(dys, dy_t)
        chips_send(c)
        for d in range(2, far):
            ahead(c + 1, d)
        if c >= 1:
            relay(c - 1)
        if c >= 2:
            for d in range(far - 1, 1, -1):
                chain(c - 2, d)
        if c + 1 < parts:
            projects(c + 1, 0)
            projects(c + 1, 1)
        if c >= 1:
            grads_of(c - 1)
        if c >= 2:
            chain(c - 2, 1)
        if c + 1 < parts:
            for d in range(2, far):
                projects(c + 1, d)
        home(c)
        spread(c)
    last = parts - 1
    if parts >= 2:
        for d in range(far - 1, 1, -1):
            chain(last - 1, d)
    relay(last)
    if parts >= 2:
        chain(last - 1, 1)
    grads_of(last)
    for r in range(1, nt):
        t = lax.rem(me + r, nt)
        start(None, pt.at[slot_of(t)], gt_ref.at[:, own_cols], psend.at[r], precv.at[mine], z, t)
    gt_ref[:, own_cols] = pt[mine]
    for d in range(far - 1, 0, -1):
        chain(last, d)
    for c in range(parts - 1):
        finish(c)
    for r in range(1, nt):
        t = lax.rem(me + r, nt)
        cols = pl.ds(pl.multiple_of(t * ds, ds), ds)
        arrived(gt_ref.at[:, cols], precv.at[slot_of(t)])
    finish(last)
    for cond, copy in pending:
        if cond is None:
            copy.wait_send()
        else:
            pl.when(cond)(copy.wait_send)


def on_device_kernel(nz, nt, tokens, grad_out, probs, routes, w_gate, w_up, w_down_t):
    rows, width = tokens.shape
    ds, f = w_gate.shape[1], w_gate.shape[2]
    f32, bf16 = jnp.float32, jnp.bfloat16
    weight = probs.astype(f32).T[:, :, None]
    route = jnp.broadcast_to(jnp.pad(routes[0], (0, 6))[:, None], (8, 3 * LANES))
    chips = nt // 2
    parts, bw = f // LANES, 3 * LANES
    vmem, dma = pltpu.VMEM, pltpu.SemaphoreType.DMA
    grad = jax.ShapeDtypeStruct((1, ds, f), f32)
    flops = 2 * nt * rows * ds * f * nz * 8
    out = pl.pallas_call(
        functools.partial(exchange_kernel, nz, nt),
        out_shape=(
            jax.ShapeDtypeStruct((rows, width), bf16),
            jax.ShapeDtypeStruct((2, rows, 1), f32),
            grad, grad, grad,
        ),
        in_specs=[pl.BlockSpec(memory_space=vmem)] * 7,
        out_specs=[pl.BlockSpec(memory_space=vmem)] * 5,
        scratch_shapes=[
            vmem((nt, rows, ds), bf16), vmem((nt, rows, ds), bf16), vmem((nt, 8, bw), jnp.int32),
            vmem((ds, nt * rows), bf16), vmem((ds, nt * rows), bf16),
            vmem((parts, ds, bw), bf16), vmem((parts, nz, ds, bw), bf16),
            vmem((parts, nt, 2, rows, bw), f32),
            vmem((parts, chips, 2, rows, bw), f32),
            vmem((parts, chips, 2, rows, bw), bf16),
            vmem((parts, chips, 2, rows, bw), bf16),
            vmem((parts, nt, 2, rows, bw), bf16),
            vmem((nz, nt, rows, bw), bf16),
            vmem((2, nz, ds, bw), f32),
            vmem((parts, nz, ds, bw), bf16), vmem((parts, nz, ds, bw), bf16), vmem((parts, ds, bw), bf16),
            vmem((nt, rows, ds), bf16), vmem((nt, rows, ds), f32),
            dma((nt,)), dma((nt,)), dma((nt,)), dma((nt,)), dma((nt,)), dma((nt,)),
            dma((2 * parts * nz,)), dma((parts * nz,)),
            dma((parts,)), dma((parts,)),
            dma((parts * chips,)), dma((parts * chips,)),
            dma((parts * nt,)), dma((parts * nt,)),
            dma((2 * parts * nz,)), dma((parts * nz,)), dma((parts,)),
            dma((nt,)), dma((nt,)),
        ],
        compiler_params=pltpu.CompilerParams(
            collective_id=0, has_side_effects=True, vmem_limit_bytes=62 * 2**20
        ),
        cost_estimate=pl.CostEstimate(flops=flops, bytes_accessed=2**23, transcendentals=0),
    )(tokens, grad_out, weight, route, w_gate, w_up, w_down_t)
    grad_probs = out[1][:, :, 0].T.astype(bf16)
    return (out[0], grad_probs, out[2], out[3], out[4])


def fits(mesh, tokens, routes, w_gate):
    nz, nt = mesh.shape["expert"], mesh.shape["tok"]
    devices = nz * nt
    rows, ds, f = tokens.shape[0] // devices, w_gate.shape[1] // nt, w_gate.shape[2]
    if routes.shape[0] != devices or w_gate.shape[0] != nz or nz != 4 or nt % 2:
        return False
    if rows % 16 or ds % 128 or f % 128 or nt > 8:
        return False
    return nt * rows <= 1024 and ds <= 384 and f <= 384


def solution(mesh):
    def run(tokens, grad_out, probs, routes, w_gate, w_up, w_down_t):
        body = on_device
        if fits(mesh, tokens, routes, w_gate):
            body = functools.partial(on_device_kernel, mesh.shape["expert"], mesh.shape["tok"])
        rows = P(("expert", "tok"), None)
        weights = P("expert", "tok", None)
        return jax.shard_map(
            body,
            mesh=mesh,
            in_specs=(rows, rows, rows, rows, weights, weights, weights),
            out_specs=(rows, rows, weights, weights, weights),
            check_vma=False,
        )(tokens, grad_out, probs, routes, w_gate, w_up, w_down_t)

    return run
```

```python
import functools

import jax
import jax.numpy as jnp
from jax import lax
from jax.experimental import pallas as pl
from jax.experimental.pallas import tpu as pltpu
from jax.sharding import PartitionSpec as P


def first_section(x_rows, dy_rows, p_rows, gate_w, up_w, down_w):
    gate_pre = jnp.dot(x_rows, gate_w, preferred_element_type=jnp.float32)
    up_pre = jnp.dot(x_rows, up_w, preferred_element_type=jnp.float32)
    hidden = jax.nn.silu(gate_pre) * up_pre
    back = jnp.dot(dy_rows, down_w, preferred_element_type=jnp.float32)
    score = jnp.sum(hidden * back, axis=1).astype(jnp.bfloat16)
    scaled = (p_rows.astype(jnp.float32)[:, None] * hidden).astype(jnp.bfloat16)
    grad_down = lax.dot_general(
        dy_rows, scaled, (((0,), (0,)), ((), ())), preferred_element_type=jnp.float32
    )
    return (gate_pre, up_pre, back, score, grad_down)


def second_section(x_rows, p_rows, gate_pre, up_pre, back, gate_w, up_w):
    sigmoid_gate = jax.nn.sigmoid(gate_pre)
    delta_hidden = p_rows.astype(jnp.float32)[:, None] * back
    delta_gate = (
        delta_hidden * up_pre * sigmoid_gate * (1.0 + gate_pre * (1.0 - sigmoid_gate))
    ).astype(jnp.bfloat16)
    delta_up = (delta_hidden * gate_pre * sigmoid_gate).astype(jnp.bfloat16)
    contract_rows = (((0,), (0,)), ((), ()))
    grad_gate = lax.dot_general(
        x_rows, delta_gate, contract_rows, preferred_element_type=jnp.float32
    )
    grad_up = lax.dot_general(x_rows, delta_up, contract_rows, preferred_element_type=jnp.float32)
    contract_cols = (((1,), (1,)), ((), ()))
    part = (
        lax.dot_general(delta_gate, gate_w, contract_cols, preferred_element_type=jnp.float32)
        + lax.dot_general(delta_up, up_w, contract_cols, preferred_element_type=jnp.float32)
    ).astype(jnp.bfloat16)
    return (grad_gate, grad_up, part)


def on_device(tokens, grad_out, probs, routes, w_gate, w_up, w_down_t):
    groups = lax.axis_size("expert")
    tile_count = routes.shape[0]
    row_count = tokens.shape[0]
    tile_rows = row_count // tile_count
    model_width = tokens.shape[1]
    gate_full, up_full, down_full = (
        lax.all_gather(w_gate, "tok", axis=1, tiled=True),
        lax.all_gather(w_up, "tok", axis=1, tiled=True),
        lax.all_gather(w_down_t, "tok", axis=1, tiled=True),
    )
    gate_w = gate_full[0]
    up_w = up_full[0]
    down_w = down_full[0]
    targets = jnp.arange(groups, dtype=jnp.int32)
    chosen = routes[None, :, :] == targets[:, None, None]
    routed = jnp.any(chosen, axis=2)
    token_tiles = tokens.reshape(tile_count, tile_rows, model_width)
    grad_tiles = grad_out.reshape(tile_count, tile_rows, model_width)
    prob_tiles = probs.reshape(tile_count, tile_rows, 2).astype(jnp.float32)
    x_send = jnp.where(routed[:, :, None, None], token_tiles[None], jnp.zeros((), jnp.bfloat16))
    dy_send = jnp.where(routed[:, :, None, None], grad_tiles[None], jnp.zeros((), jnp.bfloat16))
    p_send = jnp.sum(jnp.where(chosen[:, :, None, :], prob_tiles[None], 0.0), axis=3).astype(
        jnp.bfloat16
    )
    x_recv, dy_recv, p_recv = (
        lax.all_to_all(x_send, "expert", split_axis=0, concat_axis=0, tiled=True),
        lax.all_to_all(dy_send, "expert", split_axis=0, concat_axis=0, tiled=True),
        lax.all_to_all(p_send, "expert", split_axis=0, concat_axis=0, tiled=True),
    )
    slot_count = groups * tile_count
    x_slots = x_recv.reshape(slot_count, tile_rows, model_width)
    dy_slots = dy_recv.reshape(slot_count, tile_rows, model_width)
    p_slots = p_recv.reshape(slot_count, tile_rows)
    total_rows = slot_count * tile_rows
    gate_pre, up_pre, back, score, grad_down = first_section(
        x_slots.reshape(total_rows, model_width),
        dy_slots.reshape(total_rows, model_width),
        p_slots.reshape(total_rows),
        gate_w,
        up_w,
        down_w,
    )
    grad_gate, grad_up, part = second_section(
        x_slots.reshape(total_rows, model_width),
        p_slots.reshape(total_rows),
        gate_pre,
        up_pre,
        back,
        gate_w,
        up_w,
    )
    grad_gate_out, grad_up_out, grad_down_t = (
        lax.psum_scatter(grad_gate[None], "tok", scatter_dimension=1, tiled=True),
        lax.psum_scatter(grad_up[None], "tok", scatter_dimension=1, tiled=True),
        lax.psum_scatter(grad_down[None], "tok", scatter_dimension=1, tiled=True),
    )
    part_send = part.reshape(groups, tile_count, tile_rows, model_width)
    score_send = score.reshape(groups, tile_count, tile_rows)
    part_back, score_back = (
        lax.all_to_all(part_send, "expert", split_axis=0, concat_axis=0, tiled=True),
        lax.all_to_all(score_send, "expert", split_axis=0, concat_axis=0, tiled=True),
    )
    grad_tokens = (
        jnp.sum(part_back.astype(jnp.float32), axis=0)
        .reshape(row_count, model_width)
        .astype(jnp.bfloat16)
    )
    onehot = chosen.astype(jnp.float32)
    grad_probs = jnp.einsum("gtk,gtr->trk", onehot, score_back.astype(jnp.float32))
    grad_probs = grad_probs.reshape(row_count, 2).astype(jnp.bfloat16)
    return (grad_tokens, grad_probs, grad_gate_out, grad_up_out, grad_down_t)


LANES = 128

def exchange_kernel(
    nz, nt, x_ref, dy_ref, p_ref, r_ref, wg_ref, wu_ref, wd_ref,
    gt_ref, score_ref, gg_ref, gu_ref, gd_ref,
    pw, sacc, xs, dys, rt, x_t, dy_t, own, wall, acc, sib, comb, pin, dall, picked, gp, rout, rin, rin2, pt, ptf,
    xsend, xrecv, dsend, drecv, rsend, rrecv, wsend, wrecv, csend, crecv, hsend, hrecv,
    asend, arecv, zsend, zrecv, zrecv2, psend, precv,
):
    f32, bf16 = jnp.float32, jnp.bfloat16
    z, me = lax.axis_index("expert"), lax.axis_index("tok")
    chips = nt // 2
    chip, core = me // 2, lax.rem(me, 2)
    mine = core * chips + chip
    sibling = 2 * chip + 1 - core
    rows, ds, f = xs.shape[1], xs.shape[2], wg_ref.shape[2]
    fc = LANES
    parts, bw = f // fc, 3 * fc
    weights = (wg_ref, wu_ref, wd_ref)
    grads = (gg_ref, gu_ref, gd_ref)
    pending = []
    for c in range(parts):
        for m in range(3):
            own[c, :, m * fc : (m + 1) * fc] = weights[m][0, :, c * fc : (c + 1) * fc]

    def slot_of(tok):
        return lax.rem(tok, 2) * chips + tok // 2

    def partner(j):
        return lax.rem(chip + j, chips)

    def move(src, dst, send, recv, zz, tok):
        return pltpu.make_async_remote_copy(
            src_ref=src, dst_ref=dst, send_sem=send, recv_sem=recv,
            device_id=(zz, tok), device_id_type=pl.DeviceIdType.MESH,
        )

    def start(cond, *args):
        copy = move(*args)
        if cond is None:
            copy.start()
        else:
            pl.when(cond)(lambda: copy.start())
        pending.append((cond, copy))

    def arrived(dst, recv):
        move(dst, dst, xsend.at[0], recv, z, sibling).wait_recv()

    barrier = pltpu.get_barrier_semaphore()
    for r in range(1, nt):
        pl.semaphore_signal(
            barrier, inc=1, device_id=(z, lax.rem(me + r, nt)), device_id_type=pl.DeviceIdType.MESH
        )

    @pl.when(z > 0)
    def _():
        pl.semaphore_signal(barrier, inc=1, device_id=(z - 1, me), device_id_type=pl.DeviceIdType.MESH)

    @pl.when(z < nz - 1)
    def _():
        pl.semaphore_signal(barrier, inc=1, device_id=(z + 1, me), device_id_type=pl.DeviceIdType.MESH)

    along = jnp.where(z > 0, 1, 0) + jnp.where(z < nz - 1, 1, 0)
    pl.semaphore_wait(barrier, nt - 1 + along)

    def from_left(d):
        return (z - d >= 0) & (z < nz - 1)

    def from_right(d):
        return (z + d < nz) & (z > 0)

    def send_weight(c, d):
        src_r, src_l = wall.at[c, z - d], wall.at[c, z + d]
        base = c * 2 * nz + d
        start(from_left(d), src_r, wall.at[c, z - d], wsend.at[base], wrecv.at[c * nz + z - d], z + 1, me)
        start(from_right(d), src_l, wall.at[c, z + d], wsend.at[base + nz], wrecv.at[c * nz + z + d], z - 1, me)

    def send_own(c, cond):
        start(cond & from_left(0), own.at[c], wall.at[c, z], wsend.at[c * 2 * nz], wrecv.at[c * nz + z], z + 1, me)
        start(cond & from_right(0), own.at[c], wall.at[c, z], wsend.at[c * 2 * nz + nz],
              wrecv.at[c * nz + z], z - 1, me)

    def weight_left(c, d):
        arrived(wall.at[c, z - d], wrecv.at[c * nz + z - d])

    def weight_right(c, d):
        arrived(wall.at[c, z + d], wrecv.at[c * nz + z + d])

    def forward(c, d):
        pl.when(from_left(d))(lambda: weight_left(c, d))
        pl.when(from_right(d))(lambda: weight_right(c, d))
        send_weight(c, d)

    def take_weight(c, d):
        pl.when((z - d >= 0) & ((z == nz - 1) | (d == nz - 1)))(lambda: weight_left(c, d))
        pl.when((z + d < nz) & ((z == 0) | (d == nz - 1)))(lambda: weight_right(c, d))

    def send_rows(src_ref, dst, send, recv):
        for r in range(1, nt):
            t = lax.rem(me + r, nt)
            cols = pl.ds(pl.multiple_of(t * ds, ds), ds)
            start(None, src_ref.at[:, cols], dst.at[mine], send.at[r], recv.at[mine], z, t)

    own_cols = pl.ds(pl.multiple_of(me * ds, ds), ds)
    send_own(0, z >= 0)
    row = lax.broadcasted_iota(jnp.int32, (8, bw), 0)
    rt[mine] = jnp.where(row == 0, r_ref[0, 0], r_ref[0, 1])
    for r in range(1, nt):
        t = lax.rem(me + r, nt)
        start(None, rt.at[mine], rt.at[mine], rsend.at[r], rrecv.at[mine], z, t)
    send_rows(x_ref, xs, xsend, xrecv)
    send_rows(dy_ref, dys, dsend, drecv)
    for c in range(parts):
        wall[c, z] = own[c]
    for k in range(2):
        pw[k] = jnp.broadcast_to(p_ref[k : k + 1, :].astype(f32), (fc, rows)).T
    xs[mine] = x_ref[:, own_cols]
    dys[mine] = dy_ref[:, own_cols]

    def take_rows(dst, recv):
        for r in range(1, nt):
            s = slot_of(lax.rem(me + r, nt))
            arrived(dst.at[s], recv.at[s])

    def hits(i, k, e):
        return jnp.broadcast_to(rt[pl.ds(2 * i, 2), k : k + 1, :], (2, rows, bw)) == e

    def project(c, e, first):
        @pl.loop(0, nt // 2)
        def _(i):
            x = xs[pl.ds(2 * i, 2)].reshape(2 * rows, ds)
            dy = dys[pl.ds(2 * i, 2)].reshape(2 * rows, ds)
            up = jnp.dot(x, wall[c, e, :, : 2 * fc], preferred_element_type=f32)
            back = jnp.dot(dy, wall[c, e, :, 2 * fc :], preferred_element_type=f32)
            out = jnp.concatenate([up, back], axis=1).reshape(2, rows, bw)
            for k in range(2):
                old = jnp.zeros((2, rows, bw), f32) if first else acc[c, pl.ds(2 * i, 2), k]
                acc[c, pl.ds(2 * i, 2), k] = jnp.where(hits(i, k, e), out, old)

    def projects(c, d):
        if d == 0:
            project(c, z, True)
            return
        if (c, d) != (0, 1):
            take_weight(c, d)
        pl.when(z - d >= 0)(lambda: project(c, z - d, False))
        pl.when(z + d < nz)(lambda: project(c, z + d, False))

    def cores_send(m):
        start(None, acc.at[m, pl.ds((1 - core) * chips, chips)], sib.at[m], csend.at[m], crecv.at[m], z, sibling)

    def chips_send(m):
        arrived(sib.at[m], crecv.at[m])
        for j in range(1, chips):
            q = partner(j)
            comb[m, q] = (acc[m, core * chips + q] + sib[m, q]).astype(bf16)
            n = m * chips + j
            start(None, comb.at[m, q], pin.at[m, chip], hsend.at[n], hrecv.at[m * chips + chip], z, 2 * q + core)

    def home(c):
        for j in range(1, chips):
            q = partner(j)
            arrived(pin.at[c, q], hrecv.at[c * chips + q])
        for k in range(2):
            total = acc[c, mine, k] + sib[c, chip, k]
            for j in range(1, chips):
                total = total + pin[c, partner(j), k].astype(f32)
            g, u, b = total[:, :fc], total[:, fc : 2 * fc], total[:, 2 * fc :]
            s = jax.nn.sigmoid(g)
            hidden = g * s * u
            sacc[k] = hidden * b if c == 0 else sacc[k] + hidden * b
            scaled_back = pw[k] * b
            dall[c, mine, k, :, :fc] = (scaled_back * u * s * (1.0 + g * (1.0 - s))).astype(bf16)
            dall[c, mine, k, :, fc : 2 * fc] = (scaled_back * g * s).astype(bf16)
            dall[c, mine, k, :, 2 * fc :] = (pw[k] * hidden).astype(bf16)

    def spread(m):
        for j in range(1, chips):
            q = partner(j)
            start(None, dall.at[m, mine], dall.at[m, mine], asend.at[m * nt + j], arecv.at[m * nt + mine],
                  z, 2 * q + core)
        start(None, dall.at[m, mine], dall.at[m, mine], asend.at[m * nt], arecv.at[m * nt + mine], z, sibling)

    def relay(m):
        for j in range(1, chips):
            s = core * chips + partner(j)
            arrived(dall.at[m, s], arecv.at[m * nt + s])
            start(None, dall.at[m, s], dall.at[m, s], asend.at[m * nt + chips + j], arecv.at[m * nt + s], z, sibling)

    def gathered(m):
        for q in range(chips):
            s = (1 - core) * chips + q
            arrived(dall.at[m, s], arecv.at[m * nt + s])

    def pick(c):
        @pl.loop(0, nt // 2)
        def _(i):
            one = dall[c, pl.ds(2 * i, 2), 0].astype(f32)
            two = dall[c, pl.ds(2 * i, 2), 1].astype(f32)
            for e in range(nz):
                value = jnp.where(hits(i, 0, e), one, jnp.where(hits(i, 1, e), two, 0.0))
                picked[e, pl.ds(2 * i, 2)] = value.astype(bf16)

    def grad_of(c, e):
        up = picked[e, :, :, : 2 * fc].reshape(nt * rows, 2 * fc)
        down = picked[e, :, :, 2 * fc :].reshape(nt * rows, fc)
        gp[c % 2, e, :, : 2 * fc] = jnp.dot(x_t[...], up, preferred_element_type=f32)
        gp[c % 2, e, :, 2 * fc :] = jnp.dot(dy_t[...], down, preferred_element_type=f32)

    def chain(c, d):
        @pl.when(z + d < nz)
        def _():
            e = z + d

            @pl.when(z > 0)
            def _():
                arrived(rin.at[c, e], zrecv.at[c * nz + e])
                rout[c, e] = (gp[c % 2, e] + rin[c, e].astype(f32)).astype(bf16)

            @pl.when(z == 0)
            def _():
                rout[c, e] = gp[c % 2, e].astype(bf16)

        start(z + d < nz, rout.at[c, z + d], rin.at[c, z + d], zsend.at[c * 2 * nz + d],
              zrecv.at[c * nz + z + d], z + 1, me)

        @pl.when(z - d >= 0)
        def _():
            e = z - d

            @pl.when(z < nz - 1)
            def _():
                arrived(rin.at[c, e], zrecv.at[c * nz + e])
                rout[c, e] = (gp[c % 2, e] + rin[c, e].astype(f32)).astype(bf16)

            @pl.when(z == nz - 1)
            def _():
                rout[c, e] = gp[c % 2, e].astype(bf16)

        dst = rin2.at[c] if d == 1 else rin.at[c, z - d]
        sem = zrecv2.at[c] if d == 1 else zrecv.at[c * nz + z - d]
        start(z - d >= 0, rout.at[c, z - d], dst, zsend.at[c * 2 * nz + nz + d], sem, z - 1, me)

    def grads_of(c):
        gathered(c)
        pick(c)
        for d in range(nz - 1, 0, -1):
            pl.when(z + d < nz)(lambda d=d: grad_of(c, z + d))
            pl.when(z - d >= 0)(lambda d=d: grad_of(c, z - d))
            if d == nz - 1:
                chain(c, d)
        grad_of(c, z)
        for m in range(3):
            grads[m][0, :, c * fc : (c + 1) * fc] = gp[c % 2, z, :, m * fc : (m + 1) * fc]

        @pl.loop(0, nt // 2)
        def _(i):
            total = jnp.zeros((2 * rows, ds), f32)
            for e in range(nz):
                block = picked[e, pl.ds(2 * i, 2), :, : 2 * fc].reshape(2 * rows, 2 * fc)
                total = total + lax.dot_general(
                    block, wall[c, e, :, : 2 * fc], (((1,), (1,)), ((), ())), preferred_element_type=f32
                )
            total = total.reshape(2, rows, ds)
            if c > 0:
                total = total + ptf[pl.ds(2 * i, 2)]
            if c < parts - 1:
                ptf[pl.ds(2 * i, 2)] = total
            else:
                pt[pl.ds(2 * i, 2)] = total.astype(bf16)

    def finish(c):
        @pl.when(z > 0)
        def _():
            arrived(rin.at[c, z], zrecv.at[c * nz + z])
            for m in range(3):
                grads[m][0, :, c * fc : (c + 1) * fc] += rin[c, z, :, m * fc : (m + 1) * fc].astype(f32)

        @pl.when(z < nz - 1)
        def _():
            arrived(rin2.at[c], zrecv2.at[c])
            for m in range(3):
                grads[m][0, :, c * fc : (c + 1) * fc] += rin2[c, :, m * fc : (m + 1) * fc].astype(f32)

    def transpose(src, dst):
        for t in range(nt):
            dst[:, t * rows : (t + 1) * rows] = src[t].T

    far = nz - 1

    def ahead(c, d):
        if c < parts and d < far:
            forward(c, d)
        if c + 1 < parts and d == far - 1:
            send_own(c + 1, inner)

    inner = (z > 0) & (z < nz - 1)
    edge = (z == 0) | (z == nz - 1)
    for d in range(1, far):
        ahead(0, d)
    take_weight(0, 1)
    if parts > 1:
        send_own(1, edge)
    take_rows(rt, rrecv)
    take_rows(xs, xrecv)
    take_rows(dys, drecv)
    projects(0, 0)
    ahead(1, 1)
    for c in range(2, parts):
        send_own(c, edge)
    for d in range(1, far):
        projects(0, d)
    for c in range(parts):
        for d in range(2, far):
            ahead(c + 1, d)
        projects(c, far)
        cores_send(c)
        if c == 0:
            transpose(xs, x_t)
            transpose(dys, dy_t)
        chips_send(c)
        if c >= 1:
            relay(c - 1)
        if c >= 2:
            for d in range(far - 1, 1, -1):
                chain(c - 2, d)
        if c + 1 < parts:
            projects(c + 1, 0)
            projects(c + 1, 1)
        if c >= 1:
            grads_of(c - 1)
        if c >= 2:
            chain(c - 2, 1)
        if c + 1 < parts:
            for d in range(2, far):
                projects(c + 1, d)
        ahead(c + 2, 1)
        home(c)
        spread(c)
    last = parts - 1
    if parts >= 2:
        for d in range(far - 1, 1, -1):
            chain(last - 1, d)
    relay(last)
    if parts >= 2:
        chain(last - 1, 1)
    grads_of(last)
    for r in range(1, nt):
        t = lax.rem(me + r, nt)
        start(None, pt.at[slot_of(t)], gt_ref.at[:, own_cols], psend.at[r], precv.at[mine], z, t)
    gt_ref[:, own_cols] = pt[mine]
    score = [jnp.sum(sacc[k].T, axis=0, keepdims=True) for k in range(2)]
    score_ref[...] = jnp.concatenate(score, axis=0).astype(bf16)
    for d in range(far - 1, 0, -1):
        chain(last, d)
    for c in range(parts - 1):
        finish(c)
    for r in range(1, nt):
        t = lax.rem(me + r, nt)
        cols = pl.ds(pl.multiple_of(t * ds, ds), ds)
        arrived(gt_ref.at[:, cols], precv.at[slot_of(t)])
    finish(last)
    for cond, copy in pending:
        if cond is None:
            copy.wait_send()
        else:
            pl.when(cond)(copy.wait_send)


def place_kernel(*refs):
    copies = [pltpu.make_async_copy(refs[n], refs[5 + n], refs[10].at[n]) for n in range(5)]
    for copy in copies:
        copy.start()
    for copy in copies:
        copy.wait()


def on_device_kernel(nz, nt, tokens, grad_out, probs, routes, w_gate, w_up, w_down_t):
    rows, width = tokens.shape
    ds, f = w_gate.shape[1], w_gate.shape[2]
    f32, bf16 = jnp.float32, jnp.bfloat16
    chips = nt // 2
    parts, bw = f // LANES, 3 * LANES
    vmem, dma = pltpu.VMEM, pltpu.SemaphoreType.DMA
    grad = jax.ShapeDtypeStruct((1, ds, f), f32)
    flops = 2 * nt * rows * ds * f * nz * 8
    out = pl.pallas_call(
        functools.partial(exchange_kernel, nz, nt),
        out_shape=(
            jax.ShapeDtypeStruct((rows, width), bf16),
            jax.ShapeDtypeStruct((2, rows), bf16),
            grad, grad, grad,
        ),
        in_specs=[pl.BlockSpec(memory_space=vmem)] * 3
        + [pl.BlockSpec(memory_space=pltpu.SMEM)]
        + [pl.BlockSpec(memory_space=vmem)] * 3,
        out_specs=[pl.BlockSpec(memory_space=vmem)] * 5,
        scratch_shapes=[
            vmem((2, rows, LANES), f32), vmem((2, rows, LANES), f32),
            vmem((nt, rows, ds), bf16), vmem((nt, rows, ds), bf16), vmem((nt, 8, bw), jnp.int32),
            vmem((ds, nt * rows), bf16), vmem((ds, nt * rows), bf16),
            vmem((parts, ds, bw), bf16), vmem((parts, nz, ds, bw), bf16),
            vmem((parts, nt, 2, rows, bw), f32),
            vmem((parts, chips, 2, rows, bw), f32),
            vmem((parts, chips, 2, rows, bw), bf16),
            vmem((parts, chips, 2, rows, bw), bf16),
            vmem((parts, nt, 2, rows, bw), bf16),
            vmem((nz, nt, rows, bw), bf16),
            vmem((2, nz, ds, bw), f32),
            vmem((parts, nz, ds, bw), bf16), vmem((parts, nz, ds, bw), bf16), vmem((parts, ds, bw), bf16),
            vmem((nt, rows, ds), bf16), vmem((nt, rows, ds), f32),
            dma((nt,)), dma((nt,)), dma((nt,)), dma((nt,)), dma((nt,)), dma((nt,)),
            dma((2 * parts * nz,)), dma((parts * nz,)),
            dma((parts,)), dma((parts,)),
            dma((parts * chips,)), dma((parts * chips,)),
            dma((parts * nt,)), dma((parts * nt,)),
            dma((2 * parts * nz,)), dma((parts * nz,)), dma((parts,)),
            dma((nt,)), dma((nt,)),
        ],
        compiler_params=pltpu.CompilerParams(
            collective_id=0, has_side_effects=True, vmem_limit_bytes=62 * 2**20
        ),
        cost_estimate=pl.CostEstimate(flops=flops, bytes_accessed=2**23, transcendentals=0),
    )(tokens, grad_out, probs.T, routes, w_gate, w_up, w_down_t)
    out = pl.pallas_call(
        place_kernel,
        out_shape=[jax.ShapeDtypeStruct(a.shape, a.dtype) for a in out],
        in_specs=[pl.BlockSpec(memory_space=pl.ANY)] * 5,
        out_specs=[pl.BlockSpec(memory_space=pl.ANY)] * 5,
        scratch_shapes=[dma((5,))],
        compiler_params=pltpu.CompilerParams(vmem_limit_bytes=62 * 2**20),
    )(*out)
    return (out[0], out[1].T, out[2], out[3], out[4])


def fits(mesh, tokens, routes, w_gate):
    nz, nt = mesh.shape["expert"], mesh.shape["tok"]
    devices = nz * nt
    rows, ds, f = tokens.shape[0] // devices, w_gate.shape[1] // nt, w_gate.shape[2]
    if routes.shape[0] != devices or w_gate.shape[0] != nz or nz != 4 or nt % 2:
        return False
    if rows % 16 or ds % 128 or f % 128 or nt > 8:
        return False
    return nt * rows <= 1024 and ds <= 384 and f <= 384


def solution(mesh):
    def run(tokens, grad_out, probs, routes, w_gate, w_up, w_down_t):
        body = on_device
        if fits(mesh, tokens, routes, w_gate):
            body = functools.partial(on_device_kernel, mesh.shape["expert"], mesh.shape["tok"])
        rows = P(("expert", "tok"), None)
        weights = P("expert", "tok", None)
        return jax.shard_map(
            body,
            mesh=mesh,
            in_specs=(rows, rows, rows, rows, weights, weights, weights),
            out_specs=(rows, rows, weights, weights, weights),
            check_vma=False,
        )(tokens, grad_out, probs, routes, w_gate, w_up, w_down_t)

    return run
```

```python
import functools

import jax
import jax.numpy as jnp
from jax import lax
from jax.experimental import pallas as pl
from jax.experimental.pallas import tpu as pltpu
from jax.sharding import PartitionSpec as P


def first_section(x_rows, dy_rows, p_rows, gate_w, up_w, down_w):
    gate_pre = jnp.dot(x_rows, gate_w, preferred_element_type=jnp.float32)
    up_pre = jnp.dot(x_rows, up_w, preferred_element_type=jnp.float32)
    hidden = jax.nn.silu(gate_pre) * up_pre
    back = jnp.dot(dy_rows, down_w, preferred_element_type=jnp.float32)
    score = jnp.sum(hidden * back, axis=1).astype(jnp.bfloat16)
    scaled = (p_rows.astype(jnp.float32)[:, None] * hidden).astype(jnp.bfloat16)
    grad_down = lax.dot_general(
        dy_rows, scaled, (((0,), (0,)), ((), ())), preferred_element_type=jnp.float32
    )
    return (gate_pre, up_pre, back, score, grad_down)


def second_section(x_rows, p_rows, gate_pre, up_pre, back, gate_w, up_w):
    sigmoid_gate = jax.nn.sigmoid(gate_pre)
    delta_hidden = p_rows.astype(jnp.float32)[:, None] * back
    delta_gate = (
        delta_hidden * up_pre * sigmoid_gate * (1.0 + gate_pre * (1.0 - sigmoid_gate))
    ).astype(jnp.bfloat16)
    delta_up = (delta_hidden * gate_pre * sigmoid_gate).astype(jnp.bfloat16)
    contract_rows = (((0,), (0,)), ((), ()))
    grad_gate = lax.dot_general(
        x_rows, delta_gate, contract_rows, preferred_element_type=jnp.float32
    )
    grad_up = lax.dot_general(x_rows, delta_up, contract_rows, preferred_element_type=jnp.float32)
    contract_cols = (((1,), (1,)), ((), ()))
    part = (
        lax.dot_general(delta_gate, gate_w, contract_cols, preferred_element_type=jnp.float32)
        + lax.dot_general(delta_up, up_w, contract_cols, preferred_element_type=jnp.float32)
    ).astype(jnp.bfloat16)
    return (grad_gate, grad_up, part)


def on_device(tokens, grad_out, probs, routes, w_gate, w_up, w_down_t):
    groups = lax.axis_size("expert")
    tile_count = routes.shape[0]
    row_count = tokens.shape[0]
    tile_rows = row_count // tile_count
    model_width = tokens.shape[1]
    gate_full, up_full, down_full = (
        lax.all_gather(w_gate, "tok", axis=1, tiled=True),
        lax.all_gather(w_up, "tok", axis=1, tiled=True),
        lax.all_gather(w_down_t, "tok", axis=1, tiled=True),
    )
    gate_w = gate_full[0]
    up_w = up_full[0]
    down_w = down_full[0]
    targets = jnp.arange(groups, dtype=jnp.int32)
    chosen = routes[None, :, :] == targets[:, None, None]
    routed = jnp.any(chosen, axis=2)
    token_tiles = tokens.reshape(tile_count, tile_rows, model_width)
    grad_tiles = grad_out.reshape(tile_count, tile_rows, model_width)
    prob_tiles = probs.reshape(tile_count, tile_rows, 2).astype(jnp.float32)
    x_send = jnp.where(routed[:, :, None, None], token_tiles[None], jnp.zeros((), jnp.bfloat16))
    dy_send = jnp.where(routed[:, :, None, None], grad_tiles[None], jnp.zeros((), jnp.bfloat16))
    p_send = jnp.sum(jnp.where(chosen[:, :, None, :], prob_tiles[None], 0.0), axis=3).astype(
        jnp.bfloat16
    )
    x_recv, dy_recv, p_recv = (
        lax.all_to_all(x_send, "expert", split_axis=0, concat_axis=0, tiled=True),
        lax.all_to_all(dy_send, "expert", split_axis=0, concat_axis=0, tiled=True),
        lax.all_to_all(p_send, "expert", split_axis=0, concat_axis=0, tiled=True),
    )
    slot_count = groups * tile_count
    x_slots = x_recv.reshape(slot_count, tile_rows, model_width)
    dy_slots = dy_recv.reshape(slot_count, tile_rows, model_width)
    p_slots = p_recv.reshape(slot_count, tile_rows)
    total_rows = slot_count * tile_rows
    gate_pre, up_pre, back, score, grad_down = first_section(
        x_slots.reshape(total_rows, model_width),
        dy_slots.reshape(total_rows, model_width),
        p_slots.reshape(total_rows),
        gate_w,
        up_w,
        down_w,
    )
    grad_gate, grad_up, part = second_section(
        x_slots.reshape(total_rows, model_width),
        p_slots.reshape(total_rows),
        gate_pre,
        up_pre,
        back,
        gate_w,
        up_w,
    )
    grad_gate_out, grad_up_out, grad_down_t = (
        lax.psum_scatter(grad_gate[None], "tok", scatter_dimension=1, tiled=True),
        lax.psum_scatter(grad_up[None], "tok", scatter_dimension=1, tiled=True),
        lax.psum_scatter(grad_down[None], "tok", scatter_dimension=1, tiled=True),
    )
    part_send = part.reshape(groups, tile_count, tile_rows, model_width)
    score_send = score.reshape(groups, tile_count, tile_rows)
    part_back, score_back = (
        lax.all_to_all(part_send, "expert", split_axis=0, concat_axis=0, tiled=True),
        lax.all_to_all(score_send, "expert", split_axis=0, concat_axis=0, tiled=True),
    )
    grad_tokens = (
        jnp.sum(part_back.astype(jnp.float32), axis=0)
        .reshape(row_count, model_width)
        .astype(jnp.bfloat16)
    )
    onehot = chosen.astype(jnp.float32)
    grad_probs = jnp.einsum("gtk,gtr->trk", onehot, score_back.astype(jnp.float32))
    grad_probs = grad_probs.reshape(row_count, 2).astype(jnp.bfloat16)
    return (grad_tokens, grad_probs, grad_gate_out, grad_up_out, grad_down_t)


LANES = 128

def exchange_kernel(
    nz, nt, x_ref, dy_ref, p_ref, r_ref, wg_ref, wu_ref, wd_ref,
    gt_ref, score_ref, gg_ref, gu_ref, gd_ref,
    pw, sacc, xs, dys, rt, x_t, dy_t, own, acc, sib, comb, pin, dall, picked, gp, rout, rin, rin2, pt, ptf,
    xsend, xrecv, dsend, drecv, rsend, rrecv, wsend, wrecv, csend, crecv, hsend, hrecv,
    asend, arecv, zsend, zrecv, zrecv2, psend, precv, chosen, *walls,
):
    f32, bf16 = jnp.float32, jnp.bfloat16
    z, me = lax.axis_index("expert"), lax.axis_index("tok")
    chips = nt // 2
    chip, core = me // 2, lax.rem(me, 2)
    mine = core * chips + chip
    sibling = 2 * chip + 1 - core
    rows, ds, f = xs.shape[1], xs.shape[2], wg_ref.shape[2]
    fc = LANES
    parts, bw = f // fc, 3 * fc
    weights = (wg_ref, wu_ref, wd_ref)
    grads = (gg_ref, gu_ref, gd_ref)
    pending = []
    for c in range(parts):
        for m in range(3):
            own[c, :, m * fc : (m + 1) * fc] = weights[m][0, :, c * fc : (c + 1) * fc]

    def slot_of(tok):
        return lax.rem(tok, 2) * chips + tok // 2

    def partner(j):
        return lax.rem(chip + j, chips)

    def move(src, dst, send, recv, zz, tok):
        return pltpu.make_async_remote_copy(
            src_ref=src, dst_ref=dst, send_sem=send, recv_sem=recv,
            device_id=(zz, tok), device_id_type=pl.DeviceIdType.MESH,
        )

    def start(cond, *args):
        copy = move(*args)
        if cond is None:
            copy.start()
        else:
            pl.when(cond)(lambda: copy.start())
        pending.append((cond, copy))

    def arrived(dst, recv):
        move(dst, dst, xsend.at[0], recv, z, sibling).wait_recv()

    barrier = pltpu.get_barrier_semaphore()
    for r in range(1, nt):
        pl.semaphore_signal(
            barrier, inc=1, device_id=(z, lax.rem(me + r, nt)), device_id_type=pl.DeviceIdType.MESH
        )

    @pl.when(z > 0)
    def _():
        pl.semaphore_signal(barrier, inc=1, device_id=(z - 1, me), device_id_type=pl.DeviceIdType.MESH)

    @pl.when(z < nz - 1)
    def _():
        pl.semaphore_signal(barrier, inc=1, device_id=(z + 1, me), device_id_type=pl.DeviceIdType.MESH)

    along = jnp.where(z > 0, 1, 0) + jnp.where(z < nz - 1, 1, 0)
    pl.semaphore_wait(barrier, nt - 1 + along)

    def from_left(d):
        return (z - d >= 0) & (z < nz - 1)

    def from_right(d):
        return (z + d < nz) & (z > 0)

    def send_weight(c, d):
        src_r, src_l = walls[c].at[z - d], walls[c].at[z + d]
        base = c * 2 * nz + d
        start(from_left(d), src_r, walls[c].at[z - d], wsend.at[base], wrecv.at[c * nz + z - d], z + 1, me)
        start(from_right(d), src_l, walls[c].at[z + d], wsend.at[base + nz], wrecv.at[c * nz + z + d], z - 1, me)

    def send_own(c, cond):
        start(cond & from_left(0), own.at[c], walls[c].at[z], wsend.at[c * 2 * nz], wrecv.at[c * nz + z], z + 1, me)
        start(cond & from_right(0), own.at[c], walls[c].at[z], wsend.at[c * 2 * nz + nz],
              wrecv.at[c * nz + z], z - 1, me)

    def weight_left(c, d):
        arrived(walls[c].at[z - d], wrecv.at[c * nz + z - d])

    def weight_right(c, d):
        arrived(walls[c].at[z + d], wrecv.at[c * nz + z + d])

    def forward(c, d):
        pl.when(from_left(d))(lambda: weight_left(c, d))
        pl.when(from_right(d))(lambda: weight_right(c, d))
        send_weight(c, d)

    def take_weight(c, d):
        pl.when((z - d >= 0) & ((z == nz - 1) | (d == nz - 1)))(lambda: weight_left(c, d))
        pl.when((z + d < nz) & ((z == 0) | (d == nz - 1)))(lambda: weight_right(c, d))

    def send_rows(src_ref, dst, send, recv):
        for r in range(1, nt):
            t = lax.rem(me + r, nt)
            cols = pl.ds(pl.multiple_of(t * ds, ds), ds)
            start(None, src_ref.at[:, cols], dst.at[mine], send.at[r], recv.at[mine], z, t)

    own_cols = pl.ds(pl.multiple_of(me * ds, ds), ds)
    send_own(0, z >= 0)
    row = lax.broadcasted_iota(jnp.int32, (8, bw), 0)
    rt[mine] = jnp.where(row == 0, r_ref[0, 0], r_ref[0, 1])
    for r in range(1, nt):
        t = lax.rem(me + r, nt)
        start(None, rt.at[mine], rt.at[mine], rsend.at[r], rrecv.at[mine], z, t)
    send_rows(x_ref, xs, xsend, xrecv)
    send_rows(dy_ref, dys, dsend, drecv)
    for c in range(parts):
        walls[c][z] = own[c]
    for k in range(2):
        pw[k] = jnp.broadcast_to(p_ref[k : k + 1, :].astype(f32), (fc, rows)).T
    xs[mine] = x_ref[:, own_cols]
    dys[mine] = dy_ref[:, own_cols]

    def take_rows(dst, recv):
        for r in range(1, nt):
            s = slot_of(lax.rem(me + r, nt))
            arrived(dst.at[s], recv.at[s])

    def hits(i, k, e):
        return jnp.broadcast_to(rt[pl.ds(2 * i, 2), k : k + 1, :], (2, rows, bw)) == e

    def project(c, half):
        @pl.loop(0, chips)
        def _(i):
            t = half * chips + i
            for k in range(2):
                e = chosen[2 * t + k]
                up = jnp.dot(xs[t], walls[c][e, :, : 2 * fc], preferred_element_type=f32)
                back = jnp.dot(dys[t], walls[c][e, :, 2 * fc :], preferred_element_type=f32)
                acc[c, t, k, :, : 2 * fc] = up
                acc[c, t, k, :, 2 * fc :] = back

    def cores_send(m):
        start(None, acc.at[m, pl.ds((1 - core) * chips, chips)], sib.at[m], csend.at[m], crecv.at[m], z, sibling)

    def chips_send(m):
        arrived(sib.at[m], crecv.at[m])
        for j in range(1, chips):
            q = partner(j)
            comb[m, q] = (acc[m, core * chips + q] + sib[m, q]).astype(bf16)
            n = m * chips + j
            start(None, comb.at[m, q], pin.at[m, chip], hsend.at[n], hrecv.at[m * chips + chip], z, 2 * q + core)

    def home(c):
        for j in range(1, chips):
            q = partner(j)
            arrived(pin.at[c, q], hrecv.at[c * chips + q])
        for k in range(2):
            total = acc[c, mine, k] + sib[c, chip, k]
            for j in range(1, chips):
                total = total + pin[c, partner(j), k].astype(f32)
            g, u, b = total[:, :fc], total[:, fc : 2 * fc], total[:, 2 * fc :]
            s = jax.nn.sigmoid(g)
            hidden = g * s * u
            sacc[k] = hidden * b if c == 0 else sacc[k] + hidden * b
            scaled_back = pw[k] * b
            dall[c, mine, k, :, :fc] = (scaled_back * u * s * (1.0 + g * (1.0 - s))).astype(bf16)
            dall[c, mine, k, :, fc : 2 * fc] = (scaled_back * g * s).astype(bf16)
            dall[c, mine, k, :, 2 * fc :] = (pw[k] * hidden).astype(bf16)

    def spread(m):
        for j in range(1, chips):
            q = partner(j)
            start(None, dall.at[m, mine], dall.at[m, mine], asend.at[m * nt + j], arecv.at[m * nt + mine],
                  z, 2 * q + core)
        start(None, dall.at[m, mine], dall.at[m, mine], asend.at[m * nt], arecv.at[m * nt + mine], z, sibling)

    def relay(m):
        for j in range(1, chips):
            s = core * chips + partner(j)
            arrived(dall.at[m, s], arecv.at[m * nt + s])
            start(None, dall.at[m, s], dall.at[m, s], asend.at[m * nt + chips + j], arecv.at[m * nt + s], z, sibling)

    def gathered(m):
        for q in range(chips):
            s = (1 - core) * chips + q
            arrived(dall.at[m, s], arecv.at[m * nt + s])

    def pick(c):
        @pl.loop(0, nt // 2)
        def _(i):
            one = dall[c, pl.ds(2 * i, 2), 0].astype(f32)
            two = dall[c, pl.ds(2 * i, 2), 1].astype(f32)
            for e in range(nz):
                value = jnp.where(hits(i, 0, e), one, jnp.where(hits(i, 1, e), two, 0.0))
                picked[e, pl.ds(2 * i, 2)] = value.astype(bf16)

    def grad_of(c, e):
        up = picked[e, :, :, : 2 * fc].reshape(nt * rows, 2 * fc)
        down = picked[e, :, :, 2 * fc :].reshape(nt * rows, fc)
        gp[c % 2, e, :, : 2 * fc] = jnp.dot(x_t[...], up, preferred_element_type=f32)
        gp[c % 2, e, :, 2 * fc :] = jnp.dot(dy_t[...], down, preferred_element_type=f32)

    def chain(c, d):
        @pl.when(z + d < nz)
        def _():
            e = z + d

            @pl.when(z > 0)
            def _():
                arrived(rin.at[c, e], zrecv.at[c * nz + e])
                rout[c, e] = (gp[c % 2, e] + rin[c, e].astype(f32)).astype(bf16)

            @pl.when(z == 0)
            def _():
                rout[c, e] = gp[c % 2, e].astype(bf16)

        start(z + d < nz, rout.at[c, z + d], rin.at[c, z + d], zsend.at[c * 2 * nz + d],
              zrecv.at[c * nz + z + d], z + 1, me)

        @pl.when(z - d >= 0)
        def _():
            e = z - d

            @pl.when(z < nz - 1)
            def _():
                arrived(rin.at[c, e], zrecv.at[c * nz + e])
                rout[c, e] = (gp[c % 2, e] + rin[c, e].astype(f32)).astype(bf16)

            @pl.when(z == nz - 1)
            def _():
                rout[c, e] = gp[c % 2, e].astype(bf16)

        dst = rin2.at[c] if d == 1 else rin.at[c, z - d]
        sem = zrecv2.at[c] if d == 1 else zrecv.at[c * nz + z - d]
        start(z - d >= 0, rout.at[c, z - d], dst, zsend.at[c * 2 * nz + nz + d], sem, z - 1, me)

    def grads_of(c):
        gathered(c)
        pick(c)
        for d in range(nz - 1, 0, -1):
            pl.when(z + d < nz)(lambda d=d: grad_of(c, z + d))
            pl.when(z - d >= 0)(lambda d=d: grad_of(c, z - d))
            if d == nz - 1:
                chain(c, d)
        grad_of(c, z)
        for m in range(3):
            grads[m][0, :, c * fc : (c + 1) * fc] = gp[c % 2, z, :, m * fc : (m + 1) * fc]

        @pl.loop(0, nt)
        def _(i):
            total = jnp.zeros((rows, ds), f32)
            for k in range(2):
                e = chosen[2 * i + k]
                total = total + lax.dot_general(
                    dall[c, i, k, :, : 2 * fc], walls[c][e, :, : 2 * fc], (((1,), (1,)), ((), ())),
                    preferred_element_type=f32,
                )
            if c > 0:
                total = total + ptf[i]
            if c < parts - 1:
                ptf[i] = total
            else:
                pt[i] = total.astype(bf16)

    def finish(c):
        @pl.when(z > 0)
        def _():
            arrived(rin.at[c, z], zrecv.at[c * nz + z])
            for m in range(3):
                grads[m][0, :, c * fc : (c + 1) * fc] += rin[c, z, :, m * fc : (m + 1) * fc].astype(f32)

        @pl.when(z < nz - 1)
        def _():
            arrived(rin2.at[c], zrecv2.at[c])
            for m in range(3):
                grads[m][0, :, c * fc : (c + 1) * fc] += rin2[c, :, m * fc : (m + 1) * fc].astype(f32)

    def transpose(src, dst):
        for t in range(nt):
            dst[:, t * rows : (t + 1) * rows] = src[t].T

    far = nz - 1

    def ahead(c, d):
        if c < parts and d < far:
            forward(c, d)
        if c + 1 < parts and d == far - 1:
            send_own(c + 1, inner)

    inner = (z > 0) & (z < nz - 1)
    edge = (z == 0) | (z == nz - 1)
    for d in range(1, far):
        ahead(0, d)
    take_weight(0, 1)
    if parts > 1:
        send_own(1, edge)
    take_rows(rt, rrecv)
    for t in range(nt):
        for k in range(2):
            chosen[2 * t + k] = jnp.max(rt[t, k : k + 1, :])
    take_rows(xs, xrecv)
    transpose(xs, x_t)
    take_rows(dys, drecv)
    transpose(dys, dy_t)
    ahead(1, 1)
    for c in range(2, parts):
        send_own(c, edge)
    for c in range(parts):
        for d in range(2, far):
            ahead(c + 1, d)
        for d in range(1, far + 1):
            if (c, d) != (0, 1):
                take_weight(c, d)
        project(c, 1 - core)
        cores_send(c)
        project(c, core)
        chips_send(c)
        if c >= 1:
            relay(c - 1)
        if c >= 2:
            for d in range(far - 1, 1, -1):
                chain(c - 2, d)
        if c >= 1:
            grads_of(c - 1)
        if c >= 2:
            chain(c - 2, 1)
        ahead(c + 2, 1)
        home(c)
        spread(c)
    last = parts - 1
    if parts >= 2:
        for d in range(far - 1, 1, -1):
            chain(last - 1, d)
    relay(last)
    if parts >= 2:
        chain(last - 1, 1)
    grads_of(last)
    for r in range(1, nt):
        t = lax.rem(me + r, nt)
        start(None, pt.at[slot_of(t)], gt_ref.at[:, own_cols], psend.at[r], precv.at[mine], z, t)
    gt_ref[:, own_cols] = pt[mine]
    score = [jnp.sum(sacc[k].T, axis=0, keepdims=True) for k in range(2)]
    score_ref[...] = jnp.concatenate(score, axis=0).astype(bf16)
    for d in range(far - 1, 0, -1):
        chain(last, d)
    for c in range(parts - 1):
        finish(c)
    for r in range(1, nt):
        t = lax.rem(me + r, nt)
        cols = pl.ds(pl.multiple_of(t * ds, ds), ds)
        arrived(gt_ref.at[:, cols], precv.at[slot_of(t)])
    finish(last)
    for cond, copy in pending:
        if cond is None:
            copy.wait_send()
        else:
            pl.when(cond)(copy.wait_send)


def place_kernel(*refs):
    sources, results, held, sems = refs[:5], refs[5:10], refs[10:15], refs[15]
    loads = [pltpu.make_async_copy(sources[n], held[n], sems.at[n]) for n in range(5)]
    stores = [pltpu.make_async_copy(held[n], results[n], sems.at[5 + n]) for n in range(5)]
    for load in loads:
        load.start()
    for load, store in zip(loads, stores):
        load.wait()
        store.start()
    for store in stores:
        store.wait()


def on_device_kernel(nz, nt, tokens, grad_out, probs, routes, w_gate, w_up, w_down_t):
    rows, width = tokens.shape
    ds, f = w_gate.shape[1], w_gate.shape[2]
    f32, bf16 = jnp.float32, jnp.bfloat16
    chips = nt // 2
    parts, bw = f // LANES, 3 * LANES
    vmem, dma = pltpu.VMEM, pltpu.SemaphoreType.DMA
    grad = jax.ShapeDtypeStruct((1, ds, f), f32)
    flops = 2 * nt * rows * ds * f * nz * 8
    out = pl.pallas_call(
        functools.partial(exchange_kernel, nz, nt),
        out_shape=(
            jax.ShapeDtypeStruct((rows, width), bf16),
            jax.ShapeDtypeStruct((2, rows), bf16),
            grad, grad, grad,
        ),
        in_specs=[pl.BlockSpec(memory_space=vmem)] * 3
        + [pl.BlockSpec(memory_space=pltpu.SMEM)]
        + [pl.BlockSpec(memory_space=vmem)] * 3,
        out_specs=[pl.BlockSpec(memory_space=vmem)] * 5,
        scratch_shapes=[
            vmem((2, rows, LANES), f32), vmem((2, rows, LANES), f32),
            vmem((nt, rows, ds), bf16), vmem((nt, rows, ds), bf16), vmem((nt, 8, bw), jnp.int32),
            vmem((ds, nt * rows), bf16), vmem((ds, nt * rows), bf16),
            vmem((parts, ds, bw), bf16),
            vmem((parts, nt, 2, rows, bw), f32),
            vmem((parts, chips, 2, rows, bw), f32),
            vmem((parts, chips, 2, rows, bw), bf16),
            vmem((parts, chips, 2, rows, bw), bf16),
            vmem((parts, nt, 2, rows, bw), bf16),
            vmem((nz, nt, rows, bw), bf16),
            vmem((2, nz, ds, bw), f32),
            vmem((parts, nz, ds, bw), bf16), vmem((parts, nz, ds, bw), bf16), vmem((parts, ds, bw), bf16),
            vmem((nt, rows, ds), bf16), vmem((nt, rows, ds), f32),
            dma((nt,)), dma((nt,)), dma((nt,)), dma((nt,)), dma((nt,)), dma((nt,)),
            dma((2 * parts * nz,)), dma((parts * nz,)),
            dma((parts,)), dma((parts,)),
            dma((parts * chips,)), dma((parts * chips,)),
            dma((parts * nt,)), dma((parts * nt,)),
            dma((2 * parts * nz,)), dma((parts * nz,)), dma((parts,)),
            dma((nt,)), dma((nt,)),
            pltpu.SMEM((2 * nt,), jnp.int32),
        ] + [vmem((nz, ds, bw), bf16) for _ in range(parts)],
        compiler_params=pltpu.CompilerParams(
            collective_id=0, has_side_effects=True, vmem_limit_bytes=62 * 2**20
        ),
        cost_estimate=pl.CostEstimate(flops=flops, bytes_accessed=2**23, transcendentals=0),
    )(tokens, grad_out, probs.T, routes, w_gate, w_up, w_down_t)
    out = pl.pallas_call(
        place_kernel,
        out_shape=[jax.ShapeDtypeStruct(a.shape, a.dtype) for a in out],
        in_specs=[pl.BlockSpec(memory_space=pl.ANY)] * 5,
        out_specs=[pl.BlockSpec(memory_space=pl.ANY)] * 5,
        scratch_shapes=[vmem(a.shape, a.dtype) for a in out] + [dma((10,))],
        compiler_params=pltpu.CompilerParams(vmem_limit_bytes=62 * 2**20),
    )(*out)
    return (out[0], out[1].T, out[2], out[3], out[4])


def fits(mesh, tokens, routes, w_gate):
    nz, nt = mesh.shape["expert"], mesh.shape["tok"]
    devices = nz * nt
    rows, ds, f = tokens.shape[0] // devices, w_gate.shape[1] // nt, w_gate.shape[2]
    if routes.shape[0] != devices or w_gate.shape[0] != nz or nz != 4 or nt % 2:
        return False
    if rows % 16 or ds % 128 or f % 128 or nt > 8:
        return False
    return nt * rows <= 1024 and ds <= 384 and f <= 384


def solution(mesh):
    def run(tokens, grad_out, probs, routes, w_gate, w_up, w_down_t):
        body = on_device
        if fits(mesh, tokens, routes, w_gate):
            body = functools.partial(on_device_kernel, mesh.shape["expert"], mesh.shape["tok"])
        rows = P(("expert", "tok"), None)
        weights = P("expert", "tok", None)
        return jax.shard_map(
            body,
            mesh=mesh,
            in_specs=(rows, rows, rows, rows, weights, weights, weights),
            out_specs=(rows, rows, weights, weights, weights),
            check_vma=False,
        )(tokens, grad_out, probs, routes, w_gate, w_up, w_down_t)

    return run
```

```python
import functools

import jax
import jax.numpy as jnp
from jax import lax
from jax.experimental import pallas as pl
from jax.experimental.pallas import tpu as pltpu
from jax.sharding import PartitionSpec as P


def first_section(x_rows, dy_rows, p_rows, gate_w, up_w, down_w):
    gate_pre = jnp.dot(x_rows, gate_w, preferred_element_type=jnp.float32)
    up_pre = jnp.dot(x_rows, up_w, preferred_element_type=jnp.float32)
    hidden = jax.nn.silu(gate_pre) * up_pre
    back = jnp.dot(dy_rows, down_w, preferred_element_type=jnp.float32)
    score = jnp.sum(hidden * back, axis=1).astype(jnp.bfloat16)
    scaled = (p_rows.astype(jnp.float32)[:, None] * hidden).astype(jnp.bfloat16)
    grad_down = lax.dot_general(
        dy_rows, scaled, (((0,), (0,)), ((), ())), preferred_element_type=jnp.float32
    )
    return (gate_pre, up_pre, back, score, grad_down)


def second_section(x_rows, p_rows, gate_pre, up_pre, back, gate_w, up_w):
    sigmoid_gate = jax.nn.sigmoid(gate_pre)
    delta_hidden = p_rows.astype(jnp.float32)[:, None] * back
    delta_gate = (
        delta_hidden * up_pre * sigmoid_gate * (1.0 + gate_pre * (1.0 - sigmoid_gate))
    ).astype(jnp.bfloat16)
    delta_up = (delta_hidden * gate_pre * sigmoid_gate).astype(jnp.bfloat16)
    contract_rows = (((0,), (0,)), ((), ()))
    grad_gate = lax.dot_general(
        x_rows, delta_gate, contract_rows, preferred_element_type=jnp.float32
    )
    grad_up = lax.dot_general(x_rows, delta_up, contract_rows, preferred_element_type=jnp.float32)
    contract_cols = (((1,), (1,)), ((), ()))
    part = (
        lax.dot_general(delta_gate, gate_w, contract_cols, preferred_element_type=jnp.float32)
        + lax.dot_general(delta_up, up_w, contract_cols, preferred_element_type=jnp.float32)
    ).astype(jnp.bfloat16)
    return (grad_gate, grad_up, part)


def on_device(tokens, grad_out, probs, routes, w_gate, w_up, w_down_t):
    groups = lax.axis_size("expert")
    tile_count = routes.shape[0]
    row_count = tokens.shape[0]
    tile_rows = row_count // tile_count
    model_width = tokens.shape[1]
    gate_full, up_full, down_full = (
        lax.all_gather(w_gate, "tok", axis=1, tiled=True),
        lax.all_gather(w_up, "tok", axis=1, tiled=True),
        lax.all_gather(w_down_t, "tok", axis=1, tiled=True),
    )
    gate_w = gate_full[0]
    up_w = up_full[0]
    down_w = down_full[0]
    targets = jnp.arange(groups, dtype=jnp.int32)
    chosen = routes[None, :, :] == targets[:, None, None]
    routed = jnp.any(chosen, axis=2)
    token_tiles = tokens.reshape(tile_count, tile_rows, model_width)
    grad_tiles = grad_out.reshape(tile_count, tile_rows, model_width)
    prob_tiles = probs.reshape(tile_count, tile_rows, 2).astype(jnp.float32)
    x_send = jnp.where(routed[:, :, None, None], token_tiles[None], jnp.zeros((), jnp.bfloat16))
    dy_send = jnp.where(routed[:, :, None, None], grad_tiles[None], jnp.zeros((), jnp.bfloat16))
    p_send = jnp.sum(jnp.where(chosen[:, :, None, :], prob_tiles[None], 0.0), axis=3).astype(
        jnp.bfloat16
    )
    x_recv, dy_recv, p_recv = (
        lax.all_to_all(x_send, "expert", split_axis=0, concat_axis=0, tiled=True),
        lax.all_to_all(dy_send, "expert", split_axis=0, concat_axis=0, tiled=True),
        lax.all_to_all(p_send, "expert", split_axis=0, concat_axis=0, tiled=True),
    )
    slot_count = groups * tile_count
    x_slots = x_recv.reshape(slot_count, tile_rows, model_width)
    dy_slots = dy_recv.reshape(slot_count, tile_rows, model_width)
    p_slots = p_recv.reshape(slot_count, tile_rows)
    total_rows = slot_count * tile_rows
    gate_pre, up_pre, back, score, grad_down = first_section(
        x_slots.reshape(total_rows, model_width),
        dy_slots.reshape(total_rows, model_width),
        p_slots.reshape(total_rows),
        gate_w,
        up_w,
        down_w,
    )
    grad_gate, grad_up, part = second_section(
        x_slots.reshape(total_rows, model_width),
        p_slots.reshape(total_rows),
        gate_pre,
        up_pre,
        back,
        gate_w,
        up_w,
    )
    grad_gate_out, grad_up_out, grad_down_t = (
        lax.psum_scatter(grad_gate[None], "tok", scatter_dimension=1, tiled=True),
        lax.psum_scatter(grad_up[None], "tok", scatter_dimension=1, tiled=True),
        lax.psum_scatter(grad_down[None], "tok", scatter_dimension=1, tiled=True),
    )
    part_send = part.reshape(groups, tile_count, tile_rows, model_width)
    score_send = score.reshape(groups, tile_count, tile_rows)
    part_back, score_back = (
        lax.all_to_all(part_send, "expert", split_axis=0, concat_axis=0, tiled=True),
        lax.all_to_all(score_send, "expert", split_axis=0, concat_axis=0, tiled=True),
    )
    grad_tokens = (
        jnp.sum(part_back.astype(jnp.float32), axis=0)
        .reshape(row_count, model_width)
        .astype(jnp.bfloat16)
    )
    onehot = chosen.astype(jnp.float32)
    grad_probs = jnp.einsum("gtk,gtr->trk", onehot, score_back.astype(jnp.float32))
    grad_probs = grad_probs.reshape(row_count, 2).astype(jnp.bfloat16)
    return (grad_tokens, grad_probs, grad_gate_out, grad_up_out, grad_down_t)


LANES = 128

def exchange_kernel(
    nz, nt, x_ref, dy_ref, p_ref, r_ref, wg_ref, wu_ref, wd_ref,
    gt_ref, score_ref, gg_ref, gu_ref, gd_ref,
    pw, sacc, xs, dys, rt, x_t, dy_t, own, acc, sib, comb, pin, dall, picked, gp, rout, rin, rin2, pt, ptf,
    xsend, xrecv, dsend, drecv, rsend, rrecv, wsend, wrecv, csend, crecv, hsend, hrecv,
    asend, arecv, zsend, zrecv, zrecv2, psend, precv, chosen, *walls,
):
    f32, bf16 = jnp.float32, jnp.bfloat16
    z, me = lax.axis_index("expert"), lax.axis_index("tok")
    chips = nt // 2
    chip, core = me // 2, lax.rem(me, 2)
    mine = core * chips + chip
    sibling = 2 * chip + 1 - core
    rows, ds, f = xs.shape[1], xs.shape[2], wg_ref.shape[2]
    fc = LANES
    parts, bw = f // fc, 3 * fc
    weights = (wg_ref, wu_ref, wd_ref)
    grads = (gg_ref, gu_ref, gd_ref)
    pending = []
    for c in range(parts):
        for m in range(3):
            own[c, :, m * fc : (m + 1) * fc] = weights[m][0, :, c * fc : (c + 1) * fc]

    def slot_of(tok):
        return lax.rem(tok, 2) * chips + tok // 2

    def partner(j):
        return lax.rem(chip + j, chips)

    def move(src, dst, send, recv, zz, tok):
        return pltpu.make_async_remote_copy(
            src_ref=src, dst_ref=dst, send_sem=send, recv_sem=recv,
            device_id=(zz, tok), device_id_type=pl.DeviceIdType.MESH,
        )

    def start(cond, *args):
        copy = move(*args)
        if cond is None:
            copy.start()
        else:
            pl.when(cond)(lambda: copy.start())
        pending.append((cond, copy))

    def arrived(dst, recv):
        move(dst, dst, xsend.at[0], recv, z, sibling).wait_recv()

    barrier = pltpu.get_barrier_semaphore()
    for r in range(1, nt):
        pl.semaphore_signal(
            barrier, inc=1, device_id=(z, lax.rem(me + r, nt)), device_id_type=pl.DeviceIdType.MESH
        )

    @pl.when(z > 0)
    def _():
        pl.semaphore_signal(barrier, inc=1, device_id=(z - 1, me), device_id_type=pl.DeviceIdType.MESH)

    @pl.when(z < nz - 1)
    def _():
        pl.semaphore_signal(barrier, inc=1, device_id=(z + 1, me), device_id_type=pl.DeviceIdType.MESH)

    along = jnp.where(z > 0, 1, 0) + jnp.where(z < nz - 1, 1, 0)
    pl.semaphore_wait(barrier, nt - 1 + along)

    def from_left(d):
        return (z - d >= 0) & (z < nz - 1)

    def from_right(d):
        return (z + d < nz) & (z > 0)

    def send_weight(c, d):
        src_r, src_l = walls[c].at[z - d], walls[c].at[z + d]
        base = c * 2 * nz + d
        start(from_left(d), src_r, walls[c].at[z - d], wsend.at[base], wrecv.at[c * nz + z - d], z + 1, me)
        start(from_right(d), src_l, walls[c].at[z + d], wsend.at[base + nz], wrecv.at[c * nz + z + d], z - 1, me)

    def send_own(c, cond):
        start(cond & from_left(0), own.at[c], walls[c].at[z], wsend.at[c * 2 * nz], wrecv.at[c * nz + z], z + 1, me)
        start(cond & from_right(0), own.at[c], walls[c].at[z], wsend.at[c * 2 * nz + nz],
              wrecv.at[c * nz + z], z - 1, me)

    def weight_left(c, d):
        arrived(walls[c].at[z - d], wrecv.at[c * nz + z - d])

    def weight_right(c, d):
        arrived(walls[c].at[z + d], wrecv.at[c * nz + z + d])

    def forward(c, d):
        pl.when(from_left(d))(lambda: weight_left(c, d))
        pl.when(from_right(d))(lambda: weight_right(c, d))
        send_weight(c, d)

    def take_weight(c, d):
        pl.when((z - d >= 0) & ((z == nz - 1) | (d == nz - 1)))(lambda: weight_left(c, d))
        pl.when((z + d < nz) & ((z == 0) | (d == nz - 1)))(lambda: weight_right(c, d))

    def send_rows(src_ref, dst, send, recv):
        for r in range(1, nt):
            t = lax.rem(me + r, nt)
            cols = pl.ds(pl.multiple_of(t * ds, ds), ds)
            start(None, src_ref.at[:, cols], dst.at[mine], send.at[r], recv.at[mine], z, t)

    own_cols = pl.ds(pl.multiple_of(me * ds, ds), ds)
    send_own(0, z >= 0)
    row = lax.broadcasted_iota(jnp.int32, (8, bw), 0)
    rt[mine] = jnp.where(row == 0, r_ref[0, 0], r_ref[0, 1])
    for r in range(1, nt):
        t = lax.rem(me + r, nt)
        start(None, rt.at[mine], rt.at[mine], rsend.at[r], rrecv.at[mine], z, t)
    send_rows(x_ref, xs, xsend, xrecv)
    send_rows(dy_ref, dys, dsend, drecv)
    for c in range(parts):
        walls[c][z] = own[c]
    for k in range(2):
        pw[k] = jnp.broadcast_to(p_ref[k : k + 1, :].astype(f32), (fc, rows)).T
    xs[mine] = x_ref[:, own_cols]
    dys[mine] = dy_ref[:, own_cols]

    def take_rows(dst, recv):
        for r in range(1, nt):
            s = slot_of(lax.rem(me + r, nt))
            arrived(dst.at[s], recv.at[s])

    def hits(i, k, e):
        return jnp.broadcast_to(rt[pl.ds(2 * i, 2), k : k + 1, :], (2, rows, bw)) == e

    def project(c, half):
        @pl.loop(0, chips)
        def _(i):
            t = half * chips + i
            for k in range(2):
                e = chosen[2 * t + k]
                up = jnp.dot(xs[t], walls[c][e, :, : 2 * fc], preferred_element_type=f32)
                back = jnp.dot(dys[t], walls[c][e, :, 2 * fc :], preferred_element_type=f32)
                acc[c, t, k, :, : 2 * fc] = up
                acc[c, t, k, :, 2 * fc :] = back

    def cores_send(m):
        start(None, acc.at[m, pl.ds((1 - core) * chips, chips)], sib.at[m], csend.at[m], crecv.at[m], z, sibling)

    def chips_send(m):
        arrived(sib.at[m], crecv.at[m])
        for j in range(1, chips):
            q = partner(j)
            comb[m, q] = (acc[m, core * chips + q] + sib[m, q]).astype(bf16)
            n = m * chips + j
            start(None, comb.at[m, q], pin.at[m, chip], hsend.at[n], hrecv.at[m * chips + chip], z, 2 * q + core)

    def home(c):
        for j in range(1, chips):
            q = partner(j)
            arrived(pin.at[c, q], hrecv.at[c * chips + q])
        for k in range(2):
            total = acc[c, mine, k] + sib[c, chip, k]
            for j in range(1, chips):
                total = total + pin[c, partner(j), k].astype(f32)
            g, u, b = total[:, :fc], total[:, fc : 2 * fc], total[:, 2 * fc :]
            s = jax.nn.sigmoid(g)
            hidden = g * s * u
            sacc[k] = hidden * b if c == 0 else sacc[k] + hidden * b
            scaled_back = pw[k] * b
            dall[c, mine, k, :, :fc] = (scaled_back * u * s * (1.0 + g * (1.0 - s))).astype(bf16)
            dall[c, mine, k, :, fc : 2 * fc] = (scaled_back * g * s).astype(bf16)
            dall[c, mine, k, :, 2 * fc :] = (pw[k] * hidden).astype(bf16)

    def spread(m):
        for j in range(1, chips):
            q = partner(j)
            start(None, dall.at[m, mine], dall.at[m, mine], asend.at[m * nt + j], arecv.at[m * nt + mine],
                  z, 2 * q + core)
        start(None, dall.at[m, mine], dall.at[m, mine], asend.at[m * nt], arecv.at[m * nt + mine], z, sibling)

    def relay(m):
        for j in range(1, chips):
            s = core * chips + partner(j)
            arrived(dall.at[m, s], arecv.at[m * nt + s])
            start(None, dall.at[m, s], dall.at[m, s], asend.at[m * nt + chips + j], arecv.at[m * nt + s], z, sibling)

    def gathered(m):
        for q in range(chips):
            s = (1 - core) * chips + q
            arrived(dall.at[m, s], arecv.at[m * nt + s])

    def pick(c):
        @pl.loop(0, nt // 2)
        def _(i):
            one = dall[c, pl.ds(2 * i, 2), 0].astype(f32)
            two = dall[c, pl.ds(2 * i, 2), 1].astype(f32)
            for e in range(nz):
                value = jnp.where(hits(i, 0, e), one, jnp.where(hits(i, 1, e), two, 0.0))
                picked[e, pl.ds(2 * i, 2)] = value.astype(bf16)

    def grad_of(c, e):
        up = picked[e, :, :, : 2 * fc].reshape(nt * rows, 2 * fc)
        down = picked[e, :, :, 2 * fc :].reshape(nt * rows, fc)
        gp[c % 2, e, :, : 2 * fc] = jnp.dot(x_t[...], up, preferred_element_type=f32)
        gp[c % 2, e, :, 2 * fc :] = jnp.dot(dy_t[...], down, preferred_element_type=f32)

    def pass_right(c, d, cond):
        start(cond, rout.at[c, z + d], rin.at[c, z + d], zsend.at[c * 2 * nz + d],
              zrecv.at[c * nz + z + d], z + 1, me)

    def pass_left(c, d, cond):
        dst = rin2.at[c] if d == 1 else rin.at[c, z - d]
        sem = zrecv2.at[c] if d == 1 else zrecv.at[c * nz + z - d]
        start(cond, rout.at[c, z - d], dst, zsend.at[c * 2 * nz + nz + d], sem, z - 1, me)

    def begin_chain(c, d):
        @pl.when(z == 0)
        def _():
            grad_of(c, z + d)
            rout[c, z + d] = gp[c % 2, z + d].astype(bf16)

        pass_right(c, d, z == 0)

        @pl.when(z == nz - 1)
        def _():
            grad_of(c, z - d)
            rout[c, z - d] = gp[c % 2, z - d].astype(bf16)

        pass_left(c, d, z == nz - 1)

    def add_arrived(c, e):
        arrived(rin.at[c, e], zrecv.at[c * nz + e])
        rout[c, e] = (gp[c % 2, e] + rin[c, e].astype(f32)).astype(bf16)

    def chain(c, d):
        right, left = (z > 0) & (z + d < nz), (z - d >= 0) & (z < nz - 1)
        pl.when(right)(lambda: add_arrived(c, z + d))
        pass_right(c, d, right)
        pl.when(left)(lambda: add_arrived(c, z - d))
        pass_left(c, d, left)

    def far_grads(c):
        gathered(c)
        pick(c)
        for d in range(nz - 1, 0, -1):
            begin_chain(c, d)
            pl.when((z > 0) & (z + d < nz))(lambda d=d: grad_of(c, z + d))
            pl.when((z - d >= 0) & (z < nz - 1))(lambda d=d: grad_of(c, z - d))

    def near_grads(c):
        grad_of(c, z)
        for m in range(3):
            grads[m][0, :, c * fc : (c + 1) * fc] = gp[c % 2, z, :, m * fc : (m + 1) * fc]

        @pl.loop(0, nt)
        def _(i):
            total = jnp.zeros((rows, ds), f32)
            for k in range(2):
                e = chosen[2 * i + k]
                total = total + lax.dot_general(
                    dall[c, i, k, :, : 2 * fc], walls[c][e, :, : 2 * fc], (((1,), (1,)), ((), ())),
                    preferred_element_type=f32,
                )
            if c > 0:
                total = total + ptf[i]
            if c < parts - 1:
                ptf[i] = total
            else:
                pt[i] = total.astype(bf16)

    def finish(c):
        @pl.when(z > 0)
        def _():
            arrived(rin.at[c, z], zrecv.at[c * nz + z])
            for m in range(3):
                grads[m][0, :, c * fc : (c + 1) * fc] += rin[c, z, :, m * fc : (m + 1) * fc].astype(f32)

        @pl.when(z < nz - 1)
        def _():
            arrived(rin2.at[c], zrecv2.at[c])
            for m in range(3):
                grads[m][0, :, c * fc : (c + 1) * fc] += rin2[c, :, m * fc : (m + 1) * fc].astype(f32)

    def transpose(src, dst):
        for t in range(nt):
            dst[:, t * rows : (t + 1) * rows] = src[t].T

    far = nz - 1

    def ahead(c, d):
        if c < parts and d < far:
            forward(c, d)
        if c + 1 < parts and d == far - 1:
            send_own(c + 1, inner)

    inner = (z > 0) & (z < nz - 1)
    edge = (z == 0) | (z == nz - 1)
    for d in range(1, far):
        ahead(0, d)
    take_weight(0, 1)
    if parts > 1:
        send_own(1, edge)
    take_rows(rt, rrecv)
    for t in range(nt):
        for k in range(2):
            chosen[2 * t + k] = jnp.max(rt[t, k : k + 1, :])
    take_rows(xs, xrecv)
    transpose(xs, x_t)
    take_rows(dys, drecv)
    transpose(dys, dy_t)
    ahead(1, 1)
    for c in range(2, parts):
        send_own(c, edge)
    for c in range(parts):
        for d in range(2, far):
            ahead(c + 1, d)
        for d in range(1, far + 1):
            if (c, d) != (0, 1):
                take_weight(c, d)
        project(c, 1 - core)
        cores_send(c)
        project(c, core)
        chips_send(c)
        if c >= 1:
            relay(c - 1)
        if c >= 2:
            for d in range(far - 1, 1, -1):
                chain(c - 2, d)
        if c >= 1:
            far_grads(c - 1)
        if c >= 2:
            chain(c - 2, 1)
        ahead(c + 2, 1)
        home(c)
        spread(c)
        if c >= 1:
            near_grads(c - 1)
    last = parts - 1
    relay(last)
    if parts >= 2:
        for d in range(far - 1, 0, -1):
            chain(last - 1, d)
    far_grads(last)
    near_grads(last)
    for r in range(1, nt):
        t = lax.rem(me + r, nt)
        start(None, pt.at[slot_of(t)], gt_ref.at[:, own_cols], psend.at[r], precv.at[mine], z, t)
    gt_ref[:, own_cols] = pt[mine]
    score = [jnp.sum(sacc[k].T, axis=0, keepdims=True) for k in range(2)]
    score_ref[...] = jnp.concatenate(score, axis=0).astype(bf16)
    for d in range(far - 1, 0, -1):
        chain(last, d)
    for c in range(parts - 1):
        finish(c)
    for r in range(1, nt):
        t = lax.rem(me + r, nt)
        cols = pl.ds(pl.multiple_of(t * ds, ds), ds)
        arrived(gt_ref.at[:, cols], precv.at[slot_of(t)])
    finish(last)
    for cond, copy in pending:
        if cond is None:
            copy.wait_send()
        else:
            pl.when(cond)(copy.wait_send)


def place_kernel(*refs):
    sources, results, held, sems = refs[:5], refs[5:10], refs[10:15], refs[15]
    loads = [pltpu.make_async_copy(sources[n], held[n], sems.at[n]) for n in range(5)]
    stores = [pltpu.make_async_copy(held[n], results[n], sems.at[5 + n]) for n in range(5)]
    for load in loads:
        load.start()
    for load, store in zip(loads, stores):
        load.wait()
        store.start()
    for store in stores:
        store.wait()


def on_device_kernel(nz, nt, tokens, grad_out, probs, routes, w_gate, w_up, w_down_t):
    rows, width = tokens.shape
    ds, f = w_gate.shape[1], w_gate.shape[2]
    f32, bf16 = jnp.float32, jnp.bfloat16
    chips = nt // 2
    parts, bw = f // LANES, 3 * LANES
    vmem, dma = pltpu.VMEM, pltpu.SemaphoreType.DMA
    grad = jax.ShapeDtypeStruct((1, ds, f), f32)
    flops = 2 * nt * rows * ds * f * nz * 8
    out = pl.pallas_call(
        functools.partial(exchange_kernel, nz, nt),
        out_shape=(
            jax.ShapeDtypeStruct((rows, width), bf16),
            jax.ShapeDtypeStruct((2, rows), bf16),
            grad, grad, grad,
        ),
        in_specs=[pl.BlockSpec(memory_space=vmem)] * 3
        + [pl.BlockSpec(memory_space=pltpu.SMEM)]
        + [pl.BlockSpec(memory_space=vmem)] * 3,
        out_specs=[pl.BlockSpec(memory_space=vmem)] * 5,
        scratch_shapes=[
            vmem((2, rows, LANES), f32), vmem((2, rows, LANES), f32),
            vmem((nt, rows, ds), bf16), vmem((nt, rows, ds), bf16), vmem((nt, 8, bw), jnp.int32),
            vmem((ds, nt * rows), bf16), vmem((ds, nt * rows), bf16),
            vmem((parts, ds, bw), bf16),
            vmem((parts, nt, 2, rows, bw), f32),
            vmem((parts, chips, 2, rows, bw), f32),
            vmem((parts, chips, 2, rows, bw), bf16),
            vmem((parts, chips, 2, rows, bw), bf16),
            vmem((parts, nt, 2, rows, bw), bf16),
            vmem((nz, nt, rows, bw), bf16),
            vmem((2, nz, ds, bw), f32),
            vmem((parts, nz, ds, bw), bf16), vmem((parts, nz, ds, bw), bf16), vmem((parts, ds, bw), bf16),
            vmem((nt, rows, ds), bf16), vmem((nt, rows, ds), f32),
            dma((nt,)), dma((nt,)), dma((nt,)), dma((nt,)), dma((nt,)), dma((nt,)),
            dma((2 * parts * nz,)), dma((parts * nz,)),
            dma((parts,)), dma((parts,)),
            dma((parts * chips,)), dma((parts * chips,)),
            dma((parts * nt,)), dma((parts * nt,)),
            dma((2 * parts * nz,)), dma((parts * nz,)), dma((parts,)),
            dma((nt,)), dma((nt,)),
            pltpu.SMEM((2 * nt,), jnp.int32),
        ] + [vmem((nz, ds, bw), bf16) for _ in range(parts)],
        compiler_params=pltpu.CompilerParams(
            collective_id=0, has_side_effects=True, vmem_limit_bytes=62 * 2**20
        ),
        cost_estimate=pl.CostEstimate(flops=flops, bytes_accessed=2**23, transcendentals=0),
    )(tokens, grad_out, probs.T, routes, w_gate, w_up, w_down_t)
    out = pl.pallas_call(
        place_kernel,
        out_shape=[jax.ShapeDtypeStruct(a.shape, a.dtype) for a in out],
        in_specs=[pl.BlockSpec(memory_space=pl.ANY)] * 5,
        out_specs=[pl.BlockSpec(memory_space=pl.ANY)] * 5,
        scratch_shapes=[vmem(a.shape, a.dtype) for a in out] + [dma((10,))],
        compiler_params=pltpu.CompilerParams(vmem_limit_bytes=62 * 2**20),
    )(*out)
    return (out[0], out[1].T, out[2], out[3], out[4])


def fits(mesh, tokens, routes, w_gate):
    nz, nt = mesh.shape["expert"], mesh.shape["tok"]
    devices = nz * nt
    rows, ds, f = tokens.shape[0] // devices, w_gate.shape[1] // nt, w_gate.shape[2]
    if routes.shape[0] != devices or w_gate.shape[0] != nz or nz != 4 or nt % 2:
        return False
    if rows % 16 or ds % 128 or f % 128 or nt > 8:
        return False
    return nt * rows <= 1024 and ds <= 384 and f <= 384


def solution(mesh):
    def run(tokens, grad_out, probs, routes, w_gate, w_up, w_down_t):
        body = on_device
        if fits(mesh, tokens, routes, w_gate):
            body = functools.partial(on_device_kernel, mesh.shape["expert"], mesh.shape["tok"])
        rows = P(("expert", "tok"), None)
        weights = P("expert", "tok", None)
        return jax.shard_map(
            body,
            mesh=mesh,
            in_specs=(rows, rows, rows, rows, weights, weights, weights),
            out_specs=(rows, rows, weights, weights, weights),
            check_vma=False,
        )(tokens, grad_out, probs, routes, w_gate, w_up, w_down_t)

    return run
```
